256 devices in a mesh: row: 16 (over y, x), col: 16 (over z, core).
Axes of the slice: x: 4, y: 4, z: 8, core: 2. Of those that a mesh axis runs over, the one named last changes fastest.
Arguments:
- kernel_matrix: float32 [16384, 16384], P('row', 'col'), may hold values from -2 to 2, as said below
Outputs:
- factored: float32 [16384, 16384], P('row', 'col')
The draws below stay inside these ranges and needn't reach their ends.
Inputs may be any that keep to these rules, and one draw needn't show every extreme that they name: `kernel_matrix`: the block of A's first 512 rows and columns is positive definite, read by its symmetric part.
All inputs are finite; a program needn't handle non-finite values.
Results may differ from the reference program's by a relative error of at most 0.0003.
Values sent between devices are 32-bit elements; how exact they have to be, the bound alone decides.
No kernel may reach another device: no remote copies, remote signals or barrier semaphores. Data moves between devices by JAX's collectives and lax.ppermute only.
A program may use at most 128 MiB of HBM per device.

```python
import math
import jax
import jax.numpy as jnp
from jax import lax

NB = 256
GRID_ROWS = 16
GRID_COLS = 16
N = 16384
BR = 4
BC = 4
N_ROW = 16
N_COL = 16


def draw_kernel_matrix(key, part):
    key = jax.random.fold_in(key, 11)
    key_off, key_center, key_ridge = jax.random.split(key, 3)
    blocks = jnp.arange(N, dtype=jnp.int32) // NB
    within = jnp.arange(N, dtype=jnp.int32) % NB
    nat_r = (blocks % BR * GRID_ROWS + blocks // BR) * NB + within
    nat_c = (blocks % BC * GRID_COLS + blocks // BC) * NB + within
    lead_count = 2 * NB
    values = jax.random.uniform(key_off, (N, N), jnp.float32, -1.0, 1.0)
    centers = jax.random.normal(key_center, (lead_count, 16), jnp.float32)
    ridge = jnp.exp(jax.random.uniform(key_ridge, (), jnp.float32, math.log(0.02), math.log(0.1)))
    differ = centers[:, None, :] - centers[None, :, :]
    distance = jnp.sum(differ * differ, axis=2)
    kernel = jnp.exp(distance * (-1.0 / 26.0)) + ridge * jnp.eye(lead_count, dtype=jnp.float32)
    pick_rows = jnp.minimum(nat_r, lead_count - 1)
    pick_cols = jnp.minimum(nat_c, lead_count - 1)
    inner = kernel[pick_rows][:, pick_cols]
    lead_r = (nat_r < lead_count)[:, None]
    lead_c = (nat_c < lead_count)[None, :]
    lead = lead_r & lead_c
    outer = jnp.where(lead_c, 0.25 * values, values)
    return jnp.where(lead, inner, outer).astype(jnp.float32)


def setup_inputs(seed: int = 0) -> dict:
    arg_keys = jax.random.split(jax.random.key(seed), 2)
    kernel_matrix = draw_kernel_matrix(jax.random.fold_in(arg_keys[1], 71), 0)
    return {"kernel_matrix": kernel_matrix}


def to_natural_rows(stored, parts, per):
    width = stored.shape[1]
    return stored.reshape(parts, per, NB, width).transpose(1, 0, 2, 3).reshape(N, width)

def to_stored_cols(natural, parts, per):
    width = natural.shape[1]
    return natural.reshape(per, parts, NB, width).transpose(1, 0, 2, 3).reshape(N, width)

def factor_tile(tile):
    lower = jnp.linalg.cholesky(tile)
    inverse = jax.scipy.linalg.solve_triangular(lower, jnp.eye(NB, dtype=jnp.float32), lower=True)
    return (lower, inverse)

def reference(kernel_matrix):
    high = lax.Precision.HIGHEST
    prow = N_ROW
    pcol = N_COL

    def rpos(block):
        return (block % prow * BR + block // prow) * NB

    def cpos(block):
        return (block % pcol * BC + block // pcol) * NB
    blocks = jnp.arange(N // NB, dtype=jnp.int32)
    row_nat = blocks % BR * prow + blocks // BR
    col_nat = blocks % BC * pcol + blocks // BC
    row_idx = jnp.repeat(row_nat, NB)
    col_idx = jnp.repeat(col_nat, NB)
    tile0 = kernel_matrix[rpos(0):rpos(0) + NB, cpos(0):cpos(0) + NB]
    lower0, inv0 = factor_tile(tile0)
    panel0 = jnp.dot(kernel_matrix[:, cpos(0):cpos(0) + NB].astype(jnp.float32), inv0.T.astype(jnp.float32), precision=high, preferred_element_type=jnp.float32)
    panel0 = lax.dynamic_update_slice(panel0, lower0, (rpos(0), 0))
    cross0 = to_stored_cols(to_natural_rows(panel0, prow, BR), pcol, BC)
    column1 = kernel_matrix[:, cpos(1):cpos(1) + NB] - jnp.dot(panel0.astype(jnp.float32), cross0[cpos(1):cpos(1) + NB].T.astype(jnp.float32), precision=high, preferred_element_type=jnp.float32)
    lower1, inv1 = factor_tile(column1[rpos(1):rpos(1) + NB])
    panel1 = jnp.dot(column1.astype(jnp.float32), inv1.T.astype(jnp.float32), precision=high, preferred_element_type=jnp.float32)
    panel1 = jnp.where(row_idx[:, None] < 1, jnp.float32(0.0), panel1)
    panel1 = lax.dynamic_update_slice(panel1, lower1, (rpos(1), 0))
    cross1 = to_stored_cols(to_natural_rows(panel1, prow, BR), pcol, BC)

    def one_block(pieces):
        slab, part0, part1, block = pieces
        first = slab - jnp.dot(part0.astype(jnp.float32), cross0.T.astype(jnp.float32), precision=high, preferred_element_type=jnp.float32)
        second = first - jnp.dot(part1.astype(jnp.float32), cross1.T.astype(jnp.float32), precision=high, preferred_element_type=jnp.float32)
        keep = (col_idx[None, :] >= 2) & (block >= col_idx[None, :])
        result = jnp.where(keep, second, jnp.float32(0.0))
        result = lax.dynamic_update_slice(result, part0, (0, cpos(0)))
        result = lax.dynamic_update_slice(result, part1, (0, cpos(1)))
        return result
    out = lax.map(one_block, (kernel_matrix.reshape(N // NB, NB, N), panel0.reshape(N // NB, NB, NB), panel1.reshape(N // NB, NB, NB), row_nat))
    return out.reshape(N, N)
```

```python
import jax
import jax.numpy as jnp
from jax import lax
from jax.experimental import pallas as pl
from jax.experimental.pallas import tpu as pltpu
from jax.sharding import PartitionSpec as P

NB = 256
HB = 128
HIGH = lax.Precision.HIGHEST


def dot_nt(a, b):
    return lax.dot_general(a, b, (((1,), (1,)), ((), ())), precision=HIGH, preferred_element_type=jnp.float32)


def dot_nn(a, b):
    return lax.dot_general(a, b, (((1,), (0,)), ((), ())), precision=HIGH, preferred_element_type=jnp.float32)


def dot_tn(a, b):
    return lax.dot_general(a, b, (((0,), (0,)), ((), ())), precision=HIGH, preferred_element_type=jnp.float32)


def factor_half(m_ref):
    sub = lax.broadcasted_iota(jnp.int32, (8, HB), 0)
    for b in range(HB // 8):
        lo = 8 * b
        s = m_ref[lo:lo + 8, :HB]
        v = m_ref[lo:lo + 8, HB:]
        cols = [jnp.broadcast_to(s[:, lo + j:lo + j + 1], (8, HB)) for j in range(8)]
        diag = jnp.ones((8, HB), jnp.float32)
        for j in range(8):
            d = jnp.broadcast_to(cols[j][j:j + 1, :], (8, HB))
            diag = jnp.where(sub == j, d, diag)
            if j < 7:
                f = jnp.where(sub > j, cols[j] / d, 0.0)
                for i in range(j + 1, 8):
                    cols[i] = cols[i] - f * jnp.broadcast_to(cols[i][j:j + 1, :], (8, HB))
                s = s - f * jnp.broadcast_to(s[j:j + 1, :], (8, HB))
                v = v - f * jnp.broadcast_to(v[j:j + 1, :], (8, HB))
        root = 1.0 / jnp.sqrt(diag)
        lane = lax.broadcasted_iota(jnp.int32, (8, HB), 1)
        s = jnp.where(lane >= lo + sub, s * root, 0.0)
        v = v * root
        uw = jnp.concatenate([s, v], axis=1)
        m_ref[lo:lo + 8, :] = uw
        if lo + 8 < HB:
            full = dot_tn(s, uw)
            m_ref[lo + 8:, :] = m_ref[lo + 8:, :] - full[lo + 8:, :]


def factor_kernel(a_ref, l0_ref, w0_ref, l10_ref, l1_ref, w1_ref, s_ref, m_ref):
    a00 = a_ref[0]
    a10 = a_ref[1]
    a11 = a_ref[2]
    n = 2 * NB
    s_ref[:NB, :NB] = (a00 + a00.T) * 0.5
    s_ref[:NB, NB:] = a10.T
    s_ref[NB:, NB:] = (a11 + a11.T) * 0.5
    eye = (lax.broadcasted_iota(jnp.int32, (HB, HB), 0) == lax.broadcasted_iota(jnp.int32, (HB, HB), 1)).astype(jnp.float32)
    zero = jnp.zeros((HB, HB), jnp.float32)
    outs = ((l0_ref, w0_ref), (l1_ref, w1_ref))
    for k in range(4):
        lo = k * HB
        m_ref[:, :HB] = s_ref[lo:lo + HB, lo:lo + HB]
        m_ref[:, HB:] = eye
        factor_half(m_ref)
        u = m_ref[:, :HB]
        w = m_ref[:, HB:]
        l_ref, w_ref = outs[k // 2]
        h = (k % 2) * HB
        l_ref[h:h + HB, h:h + HB] = u.T
        w_ref[h:h + HB, h:h + HB] = w
        if k < 3:
            row = dot_nn(w, s_ref[lo:lo + HB, lo + HB:])
            s_ref[lo:lo + HB, lo + HB:] = row
            s_ref[lo + HB:, lo + HB:] = s_ref[lo + HB:, lo + HB:] - dot_tn(row, row)
        if k % 2 == 1:
            cross = s_ref[lo - HB:lo, lo:lo + HB].T
            l_ref[HB:, :HB] = cross
            l_ref[:HB, HB:] = zero
            w_ref[:HB, HB:] = zero
            w_ref[HB:, :HB] = -dot_nn(w, dot_nn(cross, w_ref[:HB, :HB]))
    l10_ref[...] = s_ref[:NB, NB:n].T


def factor(lead):
    block = jax.ShapeDtypeStruct((NB, NB), jnp.float32)
    return pl.pallas_call(
        factor_kernel,
        out_shape=[block] * 5,
        in_specs=[pl.BlockSpec(memory_space=pltpu.VMEM)],
        out_specs=[pl.BlockSpec(memory_space=pltpu.VMEM)] * 5,
        scratch_shapes=[pltpu.VMEM((2 * NB, 2 * NB), jnp.float32), pltpu.VMEM((HB, 2 * HB), jnp.float32)],
        compiler_params=pltpu.CompilerParams(vmem_limit_bytes=32 * 2**20),
        cost_estimate=pl.CostEstimate(flops=200_000_000, bytes_accessed=4_000_000, transcendentals=0),
        name="factor_lead",
    )(lead)


def update_kernel(pos_ref, a_ref, gr_ref, gc_ref, l0_ref, w0_ref, l10_ref, l1_ref, w1_ref, o_ref, pc_ref, pr_ref):
    step = pl.program_id(0)
    r = pos_ref[0]
    c = pos_ref[1]
    w0 = w0_ref[...]
    w1 = w1_ref[...]
    l10 = l10_ref[...]

    def solve(g0, g1):
        p0 = dot_nt(g0, w0)
        p1 = dot_nt(g1 - dot_nt(p0, l10), w1)
        return p0, p1

    @pl.when(step == 0)
    def _():
        for m in range(4):
            g0 = gc_ref[:, 0, m].reshape(NB, NB)
            g1 = gc_ref[:, 1, m].reshape(NB, NB)
            p0, p1 = solve(g0, g1)
            pc_ref[m, :, :NB] = p0
            pc_ref[m, :, NB:] = p1

    p0, p1 = solve(gr_ref[:, 0].reshape(NB, NB), gr_ref[:, 1].reshape(NB, NB))
    pr_ref[:, :NB] = p0
    pr_ref[:, NB:] = p1
    row = r + 16 * step

    @pl.when(row == 0)
    def _():
        pr_ref[:, :NB] = l0_ref[...]
        pr_ref[:, NB:] = jnp.zeros((NB, NB), jnp.float32)

    @pl.when(row == 1)
    def _():
        pr_ref[:, NB:] = l1_ref[...]

    for m in range(4):
        col = c + 16 * m

        @pl.when(row < col)
        def _():
            o_ref[:, m * NB:(m + 1) * NB] = jnp.zeros((NB, NB), jnp.float32)

        @pl.when(row >= col)
        def _():
            o_ref[:, m * NB:(m + 1) * NB] = a_ref[:, m * NB:(m + 1) * NB] - dot_nt(pr_ref[...], pc_ref[m])

    @pl.when(c == 0)
    def _():
        o_ref[:, :NB] = pr_ref[:, :NB]

    @pl.when(c == 1)
    def _():
        o_ref[:, :NB] = pr_ref[:, NB:]


def update(pos, a, gr, gc, l0, w0, l10, l1, w1):
    whole = pl.BlockSpec(memory_space=pltpu.VMEM)
    return pl.pallas_call(
        update_kernel,
        grid=(4,),
        out_shape=jax.ShapeDtypeStruct((4 * NB, 4 * NB), jnp.float32),
        in_specs=[
            pl.BlockSpec(memory_space=pltpu.SMEM),
            pl.BlockSpec((NB, 4 * NB), lambda i: (i, 0)),
            pl.BlockSpec((2, 2, HB, NB), lambda i: (i, 0, 0, 0)),
            whole, whole, whole, whole, whole, whole,
        ],
        out_specs=pl.BlockSpec((NB, 4 * NB), lambda i: (i, 0)),
        scratch_shapes=[pltpu.VMEM((4, NB, 2 * NB), jnp.float32), pltpu.VMEM((NB, 2 * NB), jnp.float32)],
        compiler_params=pltpu.CompilerParams(vmem_limit_bytes=48 * 2**20),
        cost_estimate=pl.CostEstimate(flops=8_000_000_000, bytes_accessed=13_000_000, transcendentals=0),
        name="solve_update",
    )(pos, a, gr, gc, l0, w0, l10, l1, w1)


def per_device(a):
    r = lax.axis_index("row").astype(jnp.int32)
    c = lax.axis_index("col").astype(jnp.int32)
    z, core = c // 2, c % 2
    x = a[:, :NB]
    pieces = x.reshape(4, 16, 16, NB).transpose(1, 0, 2, 3)
    spread = lax.all_to_all(pieces, "row", 0, 0, tiled=True)
    lead = spread[0:2, 0].reshape(32, NB)

    def payload(k):
        return jnp.concatenate([spread[2 * k:2 * k + 2].reshape(HB, NB), x[k * HB:(k + 1) * HB], lead], axis=0)

    got = jnp.where(z == 0, payload(0), 0.0)
    for k in range(1, 8):
        got = got + lax.ppermute(payload(k), "col", [(h, 2 * k + h) for h in range(2)])
    col_piece = got[:HB].reshape(2, 64, NB)
    row_piece = got[HB:2 * HB]
    lead = got[2 * HB:].reshape(2, 16, NB)

    swap = [(i, i ^ 1) for i in range(16)]
    mine = lax.dynamic_index_in_dim(col_piece, core, 0, keepdims=False)
    other = lax.ppermute(lax.dynamic_index_in_dim(col_piece, 1 - core, 0, keepdims=False), "col", swap)
    col_piece = jnp.where(core == 0, jnp.stack([mine, other]), jnp.stack([other, mine]))
    gc = lax.all_gather(col_piece.reshape(2, 4, 16, NB), "row")
    gr = lax.all_gather(row_piece, "col").reshape(8, 2, HB, NB)

    lead = lax.all_to_all(jnp.broadcast_to(lead[None], (16, 2, 16, NB)), "row", 0, 0, tiled=True)
    lead = lead.transpose(1, 0, 2, 3).reshape(2, NB, NB)
    theirs = lax.ppermute(lead, "col", swap)
    lane0 = jnp.where(core == 0, lead, theirs)
    lane1 = jnp.where(core == 0, theirs, lead)
    factors = factor(jnp.concatenate([lane0, lane1[1:]], axis=0))
    return update(jnp.stack([r, c]), a, gr, gc, *factors)


def solution(mesh):
    return jax.shard_map(
        per_device,
        mesh=mesh,
        in_specs=(P("row", "col"),),
        out_specs=P("row", "col"),
        check_vma=False,
    )
```

```python
import jax
import jax.numpy as jnp
from jax import lax
from jax.experimental import pallas as pl
from jax.experimental.pallas import tpu as pltpu
from jax.sharding import PartitionSpec as P

NB = 256
HB = 128
STEP = 16
HIGH = lax.Precision.HIGHEST
F32 = jnp.float32
BF16 = jnp.bfloat16
VMEM = pl.BlockSpec(memory_space=pltpu.VMEM)
SMEM = pl.BlockSpec(memory_space=pltpu.SMEM)


def dot_nt(a, b):
    return lax.dot_general(a, b, (((1,), (1,)), ((), ())), precision=HIGH, preferred_element_type=F32)


def dot_nn(a, b):
    return lax.dot_general(a, b, (((1,), (0,)), ((), ())), precision=HIGH, preferred_element_type=F32)


def dot_tn(a, b):
    return lax.dot_general(a, b, (((0,), (0,)), ((), ())), precision=HIGH, preferred_element_type=F32)


def dot_nt_16(a, b):
    return lax.dot_general(a, b, (((1,), (1,)), ((), ())), preferred_element_type=F32)


def split3(x):
    hi = x.astype(BF16).astype(F32)
    rest = x - hi
    mid = rest.astype(BF16).astype(F32)
    return hi, mid, rest - mid


def dot_tn_short(a, b):
    ah, am, al = split3(a)
    bh, bm, bl = split3(b)
    left = jnp.concatenate([ah, ah, am, ah, al, am], axis=0).astype(BF16)
    right = jnp.concatenate([bh, bm, bh, bl, bh, bm], axis=0).astype(BF16)
    return lax.dot_general(left, right, (((0,), (0,)), ((), ())), preferred_element_type=F32)


def reciprocal(x):
    r = pl.reciprocal(x, approx=True)
    return r * (2.0 - x * r)


def inverse_root(x):
    r = lax.rsqrt(x)
    return r * (1.5 - 0.5 * x * r * r)


def factor_half(m_ref):
    sub = lax.broadcasted_iota(jnp.int32, (STEP, HB), 0)
    lane = lax.broadcasted_iota(jnp.int32, (STEP, HB), 1)
    odd = (sub & 1) == 1

    def spread(x, i):
        return jnp.broadcast_to(x[i:i + 1, :], (STEP, HB))

    for lo in range(0, HB, STEP):
        s = m_ref[lo:lo + STEP, :HB]
        v = m_ref[lo:lo + STEP, HB:]
        cols = [jnp.broadcast_to(s[:, lo + j:lo + j + 1], (STEP, HB)) for j in range(STEP)]
        first = jnp.ones((STEP, HB), F32)
        dets = first
        cross = first
        for j in range(0, STEP, 2):
            a, b, c = spread(cols[j], j), spread(cols[j], j + 1), spread(cols[j + 1], j + 1)
            det = a * c - b * b
            pair = (sub == j) | (sub == j + 1)
            first = jnp.where(pair, a, first)
            dets = jnp.where(pair, det, dets)
            cross = jnp.where(pair, b, cross)
            if j < STEP - 2:
                r = reciprocal(det)
                below = sub > j + 1
                f0 = jnp.where(below, (cols[j] * c - cols[j + 1] * b) * r, 0.0)
                f1 = jnp.where(below, (cols[j + 1] * a - cols[j] * b) * r, 0.0)
                for i in range(j + 2, STEP):
                    cols[i] = cols[i] - (f0 * spread(cols[i], j) + f1 * spread(cols[i], j + 1))
                s = s - (f0 * spread(s, j) + f1 * spread(s, j + 1))
                v = v - (f0 * spread(v, j) + f1 * spread(v, j + 1))
        ra = inverse_root(first)
        scale = jnp.where(odd, first * ra * inverse_root(dets), ra)
        mult = jnp.where(odd, cross * ra * ra, 0.0)
        s = jnp.where(lane >= lo + sub, (s - mult * pltpu.roll(s, 1, 0)) * scale, 0.0)
        v = (v - mult * pltpu.roll(v, 1, 0)) * scale
        uw = jnp.concatenate([s, v], axis=1)
        m_ref[lo:lo + STEP, :] = uw
        if lo + STEP < HB:
            full = dot_tn_short(s, uw)
            m_ref[lo + STEP:, :] = m_ref[lo + STEP:, :] - full[lo + STEP:, :]


def factor_kernel(pos_ref, mine_ref, theirs_ref, l_ref, w_ref, a_ref, s_ref, m_ref):
    lane0 = pos_ref[1] % 2 == 0
    for k in range(16):
        at = slice(16 * k, 16 * k + 16)
        mine = mine_ref[k]
        theirs = theirs_ref[k]
        a_ref[0, at, :] = jnp.where(lane0, mine[0], theirs[0])
        a_ref[1, at, :] = jnp.where(lane0, mine[1], theirs[1])
        a_ref[2, at, :] = jnp.where(lane0, theirs[1], mine[1])
    a00 = a_ref[0]
    a11 = a_ref[2]
    s_ref[:NB, :NB] = (a00 + a00.T) * 0.5
    s_ref[:NB, NB:] = a_ref[1].T
    s_ref[NB:, NB:] = (a11 + a11.T) * 0.5
    eye = (lax.broadcasted_iota(jnp.int32, (HB, HB), 0) == lax.broadcasted_iota(jnp.int32, (HB, HB), 1)).astype(F32)
    l_ref[...] = jnp.zeros((2 * NB, 2 * NB), F32)
    w_ref[...] = jnp.zeros((2 * NB, 2 * NB), F32)
    for k in range(4):
        lo = k * HB
        hi = lo + HB
        m_ref[:, :HB] = s_ref[lo:hi, lo:hi]
        m_ref[:, HB:] = eye
        factor_half(m_ref)
        w = m_ref[:, HB:]
        l_ref[lo:hi, lo:hi] = m_ref[:, :HB].T
        w_ref[lo:hi, lo:hi] = w
        if k < 3:
            row = dot_nn(w, s_ref[lo:hi, hi:])
            s_ref[lo:hi, hi:] = row
            s_ref[hi:, hi:] = s_ref[hi:, hi:] - dot_tn(row, row)
            l_ref[hi:, lo:hi] = row.T
        if k % 2 == 1:
            w_ref[lo:hi, lo - HB:lo] = -dot_nn(w, dot_nn(l_ref[lo:hi, lo - HB:lo], w_ref[lo - HB:lo, lo - HB:lo]))
    w_ref[NB:, :NB] = -dot_nn(w_ref[NB:, NB:], dot_nn(l_ref[NB:, :NB], w_ref[:NB, :NB]))


def factor(pos, mine, theirs):
    both = jax.ShapeDtypeStruct((2 * NB, 2 * NB), F32)
    return pl.pallas_call(
        factor_kernel,
        out_shape=[both] * 2,
        in_specs=[SMEM, VMEM, VMEM],
        out_specs=[VMEM] * 2,
        scratch_shapes=[
            pltpu.VMEM((3, NB, NB), F32),
            pltpu.VMEM((2 * NB, 2 * NB), F32),
            pltpu.VMEM((HB, 2 * HB), F32),
        ],
        compiler_params=pltpu.CompilerParams(vmem_limit_bytes=16 * 2**20),
        cost_estimate=pl.CostEstimate(flops=15_000_000_000, bytes_accessed=4_000_000, transcendentals=0),
        name="factor_lead",
    )(pos, mine, theirs)


def meanwhile(pos):
    def kernel(x_ref, o_ref):
        o_ref[0] = x_ref[0]
        o_ref[1] = x_ref[1]

    return pl.pallas_call(
        kernel,
        out_shape=jax.ShapeDtypeStruct(pos.shape, pos.dtype),
        in_specs=[SMEM],
        out_specs=SMEM,
        cost_estimate=pl.CostEstimate(flops=40_000_000_000, bytes_accessed=100_000_000, transcendentals=0),
        name="meanwhile",
    )(pos)


def rows_kernel(pos_ref, mine_ref, other_ref, l_ref, w_ref, p_hbm, q_hbm, p_ref, q_ref, p_sem, q_sem):
    r = pos_ref[0]
    c = pos_ref[1]
    n = 2 * NB
    lane0 = c % 2 == 0
    copies = []
    for k in range(4):
        at = slice(k * NB, (k + 1) * NB)
        mine = mine_ref[at, :]
        other = other_ref[at, :]
        g0 = jnp.where(lane0, mine, other)
        g1 = jnp.where(lane0, other, mine)
        p0 = dot_nt(g0, w_ref[:NB, :NB])
        p1 = dot_nt(jnp.concatenate([g0, g1], axis=1), w_ref[NB:, :])
        q0 = dot_nn(jnp.concatenate([p0, p1], axis=1), w_ref[:, :NB])
        q1 = dot_nn(p1, w_ref[NB:, NB:])
        for h, part in enumerate(split3(jnp.concatenate([q0, q1], axis=1))):
            q_ref[at, h * n:(h + 1) * n] = part.astype(BF16)
        copies.append(pltpu.make_async_copy(q_ref.at[at], q_hbm.at[at], q_sem.at[k]))
        copies[-1].start()
        p = jnp.where(c == 0, p0, p1)
        if k == 0:
            zero = jnp.zeros((NB, NB), F32)
            p = jnp.where(r == 0, jnp.where(c == 0, l_ref[:NB, :NB], zero), p)
            p = jnp.where(r == 1, jnp.where(c == 0, l_ref[NB:, :NB], l_ref[NB:, NB:]), p)
        p_ref[at, :] = p
    copies.append(pltpu.make_async_copy(p_ref, p_hbm, p_sem))
    copies[-1].start()
    for copy in copies:
        copy.wait()


def solve_rows(pos, mine, other, factors):
    hbm = pl.BlockSpec(memory_space=pltpu.HBM)
    p = jax.ShapeDtypeStruct((4 * NB, NB), F32)
    q = jax.ShapeDtypeStruct((4 * NB, 6 * NB), BF16)
    return pl.pallas_call(
        rows_kernel,
        out_shape=[p, q],
        in_specs=[SMEM] + [VMEM] * 4,
        out_specs=[hbm] * 2,
        scratch_shapes=[
            pltpu.VMEM(p.shape, F32),
            pltpu.VMEM(q.shape, BF16),
            pltpu.SemaphoreType.DMA(()),
            pltpu.SemaphoreType.DMA((4,)),
        ],
        compiler_params=pltpu.CompilerParams(vmem_limit_bytes=20 * 2**20),
        cost_estimate=pl.CostEstimate(flops=9_000_000_000, bytes_accessed=5_000_000, transcendentals=0),
        name="solve_rows",
    )(pos, mine, other, *factors)


def update_kernel(pos_ref, a_hbm, p_hbm, q_hbm, gc_ref, o_hbm, a_ref, p_ref, q_ref, g_ref, o_ref, sems):
    r = pos_ref[0]
    c = pos_ref[1]
    n = 2 * NB
    order = (3, 2, 1, 0)
    rows = [slice(k * NB, (k + 1) * NB) for k in range(4)]
    loads = {}
    for k in order:
        loads[k] = [
            pltpu.make_async_copy(q_hbm.at[rows[k]], q_ref.at[rows[k]], sems.at[0, k]),
            pltpu.make_async_copy(a_hbm.at[rows[k]], a_ref.at[rows[k]], sems.at[1, k]),
            pltpu.make_async_copy(p_hbm.at[rows[k]], p_ref.at[rows[k]], sems.at[2, k]),
        ]
        for copy in loads[k]:
            copy.start()

    core = c % 2
    for h, lane in enumerate((core, 1 - core)):
        for m in range(4):
            hi, mid, lo = split3(gc_ref[:, lane, m].reshape(NB, NB))
            for k, part in enumerate((lo, mid, hi)):
                g_ref[rows[m], k * n + h * NB:k * n + (h + 1) * NB] = part.astype(BF16)

    stores = []
    for k in order:
        for copy in loads[k]:
            copy.wait()
        row = r + 16 * k
        for m in range(4):
            col = c + 16 * m

            @pl.when(row < col)
            def _():
                o_ref[rows[k], rows[m]] = jnp.zeros((NB, NB), F32)

            @pl.when(row >= col)
            def _():
                small = dot_nt_16(q_ref[rows[k], :], g_ref[rows[m], :])
                small += dot_nt_16(q_ref[rows[k], :2 * n], g_ref[rows[m], n:])
                o_ref[rows[k], rows[m]] = a_ref[rows[k], rows[m]] - (
                    small + dot_nt_16(q_ref[rows[k], :n], g_ref[rows[m], 2 * n:])
                )

        @pl.when(c < 2)
        def _():
            o_ref[rows[k], :NB] = p_ref[rows[k], :]

        stores.append(pltpu.make_async_copy(o_ref.at[rows[k]], o_hbm.at[rows[k]], sems.at[3, k]))
        stores[-1].start()
    for copy in stores:
        copy.wait()


def update(pos, a, p, q, gc):
    hbm = pl.BlockSpec(memory_space=pltpu.HBM)
    return pl.pallas_call(
        update_kernel,
        out_shape=jax.ShapeDtypeStruct(a.shape, F32),
        in_specs=[SMEM, hbm, hbm, hbm, VMEM],
        out_specs=hbm,
        scratch_shapes=[
            pltpu.VMEM(a.shape, F32),
            pltpu.VMEM(p.shape, F32),
            pltpu.VMEM(q.shape, BF16),
            pltpu.VMEM(q.shape, BF16),
            pltpu.VMEM(a.shape, F32),
            pltpu.SemaphoreType.DMA((4, 4)),
        ],
        compiler_params=pltpu.CompilerParams(vmem_limit_bytes=32 * 2**20),
        cost_estimate=pl.CostEstimate(flops=8_000_000_000, bytes_accessed=13_000_000, transcendentals=0),
        name="update",
    )(pos, a, p, q, gc)


TREE = (
    tuple(((0, d or 4),) for d in range(8)),
    (
        ((0, 6), (4, 2)), ((0, 6), (1, 3)), ((0, 6), (2, 4)), ((0, 6), (3, 5)),
        ((0, 2), (4, 6)), ((0, 2), (5, 3)), ((0, 2), (6, 4)), ((0, 2), (7, 5)),
    ),
    (
        ((0, 7), (6, 5), (4, 3), (2, 1)), ((0, 7), (1, 2), (3, 4), (6, 5)),
        ((0, 1), (2, 3), (4, 5), (6, 7)), ((0, 1), (3, 2), (5, 4), (6, 7)),
        ((0, 1), (2, 3), (4, 5), (6, 7)), ((0, 7), (2, 1), (3, 4), (5, 6)),
        ((0, 1), (2, 3), (4, 5), (6, 7)), ((0, 1), (2, 3), (5, 4), (7, 6)),
    ),
)


LEAD = (((0, 5),), ((0, 7), (5, 3)), ((7, 6), (5, 4), (3, 2)), ((2, 1),))


def along_z(x, moves):
    pairs = [(16 * r + 2 * a + h, 16 * r + 2 * b + h) for r in range(16) for a, b in moves(r // 2) for h in range(2)]
    return lax.ppermute(x, ("row", "col"), pairs)


def per_device(a):
    r = lax.axis_index("row").astype(jnp.int32)
    c = lax.axis_index("col").astype(jnp.int32)
    pos = jnp.stack([r, c])
    swap = [(i, i ^ 1) for i in range(16)]
    x = a[:, :NB]
    here = c < 2

    lead = lax.all_to_all(x[:NB].reshape(16, 16, NB), "row", 0, 0, tiled=True)[0:2].reshape(32, NB)
    lead = jnp.where(here, lead, 0.0)
    for moves in LEAD:
        lead += along_z(lead, lambda d: moves if d < 5 else [((8 - s) % 8, (8 - t) % 8) for s, t in moves])
    panel = jnp.where(here, x, 0.0)
    panel += along_z(panel, lambda d: TREE[0][d])
    lead, panel, pos = lax.optimization_barrier((lead, panel, pos))

    pieces = panel.reshape(4, 16, 16, NB).transpose(1, 0, 2, 3).reshape(16, 64, NB)
    pieces = jnp.concatenate([pieces, jnp.broadcast_to(lead[None], (16, 32, NB))], axis=1)
    held = lax.all_to_all(pieces, "row", 0, 0, tiled=True)
    arrived = along_z(panel, lambda d: TREE[1][d])
    held, arrived, pos = lax.optimization_barrier((held, arrived, meanwhile(pos)))
    panel += arrived

    lead = held[:, 64:].reshape(16, 2, 16, NB)
    theirs = lax.ppermute(lead, "col", swap)
    mine = lax.dynamic_index_in_dim(held, c, 0, keepdims=False)[:64]
    other = lax.ppermute(lax.dynamic_index_in_dim(held, c ^ 1, 0, keepdims=False)[:64], "col", swap)
    mine, other, lead, theirs, panel = lax.optimization_barrier((mine, other, lead, theirs, panel))
    gc = jnp.stack([mine, other]).reshape(2, 4, 16, NB)
    gc = lax.all_to_all(jnp.broadcast_to(gc[None], (16, 2, 4, 16, NB)), "row", 0, 0, tiled=True)
    arrived = along_z(panel, lambda d: TREE[2][d])
    *factors, arrived = lax.optimization_barrier((*factor(pos, lead, theirs), arrived))
    panel += arrived
    p, q = solve_rows(pos, panel, lax.ppermute(panel, "col", swap), factors)
    return update(pos, a, p, q, gc)


def solution(mesh):
    return jax.shard_map(
        per_device,
        mesh=mesh,
        in_specs=(P("row", "col"),),
        out_specs=P("row", "col"),
        check_vma=False,
    )
```

```python
import jax
import jax.numpy as jnp
from jax import lax
from jax.experimental import pallas as pl
from jax.experimental.pallas import tpu as pltpu
from jax.sharding import PartitionSpec as P

NB = 256
HB = 128
STEP = 16
HIGH = lax.Precision.HIGHEST
F32 = jnp.float32
BF16 = jnp.bfloat16
VMEM = pl.BlockSpec(memory_space=pltpu.VMEM)
SMEM = pl.BlockSpec(memory_space=pltpu.SMEM)


def dot_nt(a, b):
    return lax.dot_general(a, b, (((1,), (1,)), ((), ())), precision=HIGH, preferred_element_type=F32)


def dot_nn(a, b):
    return lax.dot_general(a, b, (((1,), (0,)), ((), ())), precision=HIGH, preferred_element_type=F32)


def dot_tn(a, b):
    return lax.dot_general(a, b, (((0,), (0,)), ((), ())), precision=HIGH, preferred_element_type=F32)


def dot_nt_16(a, b):
    return lax.dot_general(a, b, (((1,), (1,)), ((), ())), preferred_element_type=F32)


def split3(x):
    hi = x.astype(BF16).astype(F32)
    rest = x - hi
    mid = rest.astype(BF16).astype(F32)
    return hi, mid, rest - mid


def dot_tn_short(a, b):
    ah, am, al = split3(a)
    bh, bm, bl = split3(b)
    left = jnp.concatenate([ah, ah, am, ah, al, am], axis=0).astype(BF16)
    right = jnp.concatenate([bh, bm, bh, bl, bh, bm], axis=0).astype(BF16)
    return lax.dot_general(left, right, (((0,), (0,)), ((), ())), preferred_element_type=F32)


def reciprocal(x):
    r = pl.reciprocal(x, approx=True)
    return r * (2.0 - x * r)


def inverse_root(x):
    r = lax.rsqrt(x)
    return r * (1.5 - 0.5 * x * r * r)


def factor_half(m_ref):
    sub = lax.broadcasted_iota(jnp.int32, (STEP, HB), 0)
    lane = lax.broadcasted_iota(jnp.int32, (STEP, HB), 1)
    odd = (sub & 1) == 1

    def spread(x, i):
        return jnp.broadcast_to(x[i:i + 1, :], (STEP, HB))

    for lo in range(0, HB, STEP):
        s = m_ref[lo:lo + STEP, :HB]
        v = m_ref[lo:lo + STEP, HB:]
        cols = [jnp.broadcast_to(s[:, lo + j:lo + j + 1], (STEP, HB)) for j in range(STEP)]
        first = jnp.ones((STEP, HB), F32)
        dets = first
        cross = first
        for j in range(0, STEP, 2):
            a, b, c = spread(cols[j], j), spread(cols[j], j + 1), spread(cols[j + 1], j + 1)
            det = a * c - b * b
            pair = (sub == j) | (sub == j + 1)
            first = jnp.where(pair, a, first)
            dets = jnp.where(pair, det, dets)
            cross = jnp.where(pair, b, cross)
            if j < STEP - 2:
                r = reciprocal(det)
                below = sub > j + 1
                f0 = jnp.where(below, (cols[j] * c - cols[j + 1] * b) * r, 0.0)
                f1 = jnp.where(below, (cols[j + 1] * a - cols[j] * b) * r, 0.0)
                for i in range(j + 2, STEP):
                    cols[i] = cols[i] - (f0 * spread(cols[i], j) + f1 * spread(cols[i], j + 1))
                s = s - (f0 * spread(s, j) + f1 * spread(s, j + 1))
                v = v - (f0 * spread(v, j) + f1 * spread(v, j + 1))
        ra = inverse_root(first)
        scale = jnp.where(odd, first * ra * inverse_root(dets), ra)
        mult = jnp.where(odd, cross * ra * ra, 0.0)
        s = jnp.where(lane >= lo + sub, (s - mult * pltpu.roll(s, 1, 0)) * scale, 0.0)
        v = (v - mult * pltpu.roll(v, 1, 0)) * scale
        uw = jnp.concatenate([s, v], axis=1)
        m_ref[lo:lo + STEP, :] = uw
        if lo + STEP < HB:
            full = dot_tn_short(s, uw)
            m_ref[lo + STEP:, :] = m_ref[lo + STEP:, :] - full[lo + STEP:, :]


def factor_kernel(pos_ref, mine_ref, theirs_ref, l_ref, w_ref, a_ref, s_ref, m_ref):
    lane0 = pos_ref[1] % 2 == 0
    for k in range(16):
        at = slice(16 * k, 16 * k + 16)
        mine = mine_ref[k]
        theirs = theirs_ref[k]
        a_ref[0, at, :] = jnp.where(lane0, mine[0], theirs[0])
        a_ref[1, at, :] = jnp.where(lane0, mine[1], theirs[1])
        a_ref[2, at, :] = jnp.where(lane0, theirs[1], mine[1])
    a00 = a_ref[0]
    a11 = a_ref[2]
    s_ref[:NB, :NB] = (a00 + a00.T) * 0.5
    s_ref[:NB, NB:] = a_ref[1].T
    s_ref[NB:, NB:] = (a11 + a11.T) * 0.5
    eye = (lax.broadcasted_iota(jnp.int32, (HB, HB), 0) == lax.broadcasted_iota(jnp.int32, (HB, HB), 1)).astype(F32)
    l_ref[...] = jnp.zeros((2 * NB, 2 * NB), F32)
    w_ref[...] = jnp.zeros((2 * NB, 2 * NB), F32)
    for k in range(4):
        lo = k * HB
        hi = lo + HB
        m_ref[:, :HB] = s_ref[lo:hi, lo:hi]
        m_ref[:, HB:] = eye
        factor_half(m_ref)
        w = m_ref[:, HB:]
        l_ref[lo:hi, lo:hi] = m_ref[:, :HB].T
        w_ref[lo:hi, lo:hi] = w
        if k < 3:
            row = dot_nn(w, s_ref[lo:hi, hi:])
            s_ref[lo:hi, hi:] = row
            s_ref[hi:, hi:] = s_ref[hi:, hi:] - dot_tn(row, row)
            l_ref[hi:, lo:hi] = row.T
        if k % 2 == 1:
            w_ref[lo:hi, lo - HB:lo] = -dot_nn(w, dot_nn(l_ref[lo:hi, lo - HB:lo], w_ref[lo - HB:lo, lo - HB:lo]))
    w_ref[NB:, :NB] = -dot_nn(w_ref[NB:, NB:], dot_nn(l_ref[NB:, :NB], w_ref[:NB, :NB]))


def factor(pos, mine, theirs):
    both = jax.ShapeDtypeStruct((2 * NB, 2 * NB), F32)
    return pl.pallas_call(
        factor_kernel,
        out_shape=[both] * 2,
        in_specs=[SMEM, VMEM, VMEM],
        out_specs=[VMEM] * 2,
        scratch_shapes=[
            pltpu.VMEM((3, NB, NB), F32),
            pltpu.VMEM((2 * NB, 2 * NB), F32),
            pltpu.VMEM((HB, 2 * HB), F32),
        ],
        compiler_params=pltpu.CompilerParams(vmem_limit_bytes=16 * 2**20),
        cost_estimate=pl.CostEstimate(flops=15_000_000_000, bytes_accessed=4_000_000, transcendentals=0),
        name="factor_lead",
    )(pos, mine, theirs)


def meanwhile(pos):
    def kernel(x_ref, o_ref):
        o_ref[0] = x_ref[0]
        o_ref[1] = x_ref[1]

    return pl.pallas_call(
        kernel,
        out_shape=jax.ShapeDtypeStruct(pos.shape, pos.dtype),
        in_specs=[SMEM],
        out_specs=SMEM,
        cost_estimate=pl.CostEstimate(flops=40_000_000_000, bytes_accessed=100_000_000, transcendentals=0),
        name="meanwhile",
    )(pos)


def rows_kernel(pos_ref, mine_ref, other_ref, l_ref, w_ref, p_hbm, q_hbm, p_ref, q_ref, p_sem, q_sem):
    r = pos_ref[0]
    c = pos_ref[1]
    n = 2 * NB
    lane0 = c % 2 == 0
    copies = []
    for k in range(4):
        at = slice(k * NB, (k + 1) * NB)
        mine = mine_ref[at, :]
        other = other_ref[at, :]
        g0 = jnp.where(lane0, mine, other)
        g1 = jnp.where(lane0, other, mine)
        p0 = dot_nt(g0, w_ref[:NB, :NB])
        p1 = dot_nt(jnp.concatenate([g0, g1], axis=1), w_ref[NB:, :])
        q0 = dot_nn(jnp.concatenate([p0, p1], axis=1), w_ref[:, :NB])
        q1 = dot_nn(p1, w_ref[NB:, NB:])
        for h, part in enumerate(split3(jnp.concatenate([q0, q1], axis=1))):
            q_ref[at, h * n:(h + 1) * n] = part.astype(BF16)
        copies.append(pltpu.make_async_copy(q_ref.at[at], q_hbm.at[at], q_sem.at[k]))
        copies[-1].start()
        p = jnp.where(c == 0, p0, p1)
        if k == 0:
            zero = jnp.zeros((NB, NB), F32)
            p = jnp.where(r == 0, jnp.where(c == 0, l_ref[:NB, :NB], zero), p)
            p = jnp.where(r == 1, jnp.where(c == 0, l_ref[NB:, :NB], l_ref[NB:, NB:]), p)
        p_ref[at, :] = p
    copies.append(pltpu.make_async_copy(p_ref, p_hbm, p_sem))
    copies[-1].start()
    for copy in copies:
        copy.wait()


def solve_rows(pos, mine, other, factors):
    hbm = pl.BlockSpec(memory_space=pltpu.HBM)
    p = jax.ShapeDtypeStruct((4 * NB, NB), F32)
    q = jax.ShapeDtypeStruct((4 * NB, 6 * NB), BF16)
    return pl.pallas_call(
        rows_kernel,
        out_shape=[pltpu.HBM(p.shape, F32), pltpu.HBM(q.shape, BF16)],
        in_specs=[SMEM] + [VMEM] * 4,
        out_specs=[hbm] * 2,
        scratch_shapes=[
            pltpu.VMEM(p.shape, F32),
            pltpu.VMEM(q.shape, BF16),
            pltpu.SemaphoreType.DMA(()),
            pltpu.SemaphoreType.DMA((4,)),
        ],
        compiler_params=pltpu.CompilerParams(vmem_limit_bytes=20 * 2**20),
        cost_estimate=pl.CostEstimate(flops=9_000_000_000, bytes_accessed=5_000_000, transcendentals=0),
        name="solve_rows",
    )(pos, mine, other, *factors)


def update_kernel(pos_ref, a_hbm, p_hbm, q_hbm, gc_ref, o_hbm, a_ref, p_ref, q_ref, g_ref, o_ref, sems):
    r = pos_ref[0]
    c = pos_ref[1]
    n = 2 * NB
    order = (3, 2, 1, 0)
    rows = [slice(k * NB, (k + 1) * NB) for k in range(4)]
    loads = {}
    for k in order:
        loads[k] = [
            pltpu.make_async_copy(q_hbm.at[rows[k]], q_ref.at[rows[k]], sems.at[0, k]),
            pltpu.make_async_copy(a_hbm.at[rows[k]], a_ref.at[rows[k]], sems.at[1, k]),
            pltpu.make_async_copy(p_hbm.at[rows[k]], p_ref.at[rows[k]], sems.at[2, k]),
        ]
        for copy in loads[k]:
            copy.start()

    core = c % 2
    for h, lane in enumerate((core, 1 - core)):
        for m in range(4):
            hi, mid, lo = split3(gc_ref[:, lane, m].reshape(NB, NB))
            for k, part in enumerate((lo, mid, hi)):
                g_ref[rows[m], k * n + h * NB:k * n + (h + 1) * NB] = part.astype(BF16)

    stores = []
    for k in order:
        for copy in loads[k]:
            copy.wait()
        row = r + 16 * k
        for m in range(4):
            col = c + 16 * m

            @pl.when(row < col)
            def _():
                o_ref[rows[k], rows[m]] = jnp.zeros((NB, NB), F32)

            @pl.when(row >= col)
            def _():
                small = dot_nt_16(q_ref[rows[k], :], g_ref[rows[m], :])
                small += dot_nt_16(q_ref[rows[k], :2 * n], g_ref[rows[m], n:])
                o_ref[rows[k], rows[m]] = a_ref[rows[k], rows[m]] - (
                    small + dot_nt_16(q_ref[rows[k], :n], g_ref[rows[m], 2 * n:])
                )

        @pl.when(c < 2)
        def _():
            o_ref[rows[k], :NB] = p_ref[rows[k], :]

        stores.append(pltpu.make_async_copy(o_ref.at[rows[k]], o_hbm.at[rows[k]], sems.at[3, k]))
        stores[-1].start()
    for copy in stores:
        copy.wait()


def update(pos, a, p, q, gc):
    hbm = pl.BlockSpec(memory_space=pltpu.HBM)
    return pl.pallas_call(
        update_kernel,
        out_shape=jax.ShapeDtypeStruct(a.shape, F32),
        in_specs=[SMEM, hbm, hbm, hbm, VMEM],
        out_specs=hbm,
        scratch_shapes=[
            pltpu.VMEM(a.shape, F32),
            pltpu.VMEM(p.shape, F32),
            pltpu.VMEM(q.shape, BF16),
            pltpu.VMEM(q.shape, BF16),
            pltpu.VMEM(a.shape, F32),
            pltpu.SemaphoreType.DMA((4, 4)),
        ],
        compiler_params=pltpu.CompilerParams(vmem_limit_bytes=32 * 2**20),
        cost_estimate=pl.CostEstimate(flops=8_000_000_000, bytes_accessed=13_000_000, transcendentals=0),
        name="update",
    )(pos, a, p, q, gc)


TREE = (
    tuple(((0, d or 4),) for d in range(8)),
    (
        ((0, 6), (4, 2)), ((0, 6), (1, 3)), ((0, 6), (2, 4)), ((0, 6), (3, 5)),
        ((0, 2), (4, 6)), ((0, 2), (5, 3)), ((0, 2), (6, 4)), ((0, 2), (7, 5)),
    ),
    (
        ((0, 7), (6, 5), (4, 3), (2, 1)), ((0, 7), (1, 2), (3, 4), (6, 5)),
        ((0, 1), (2, 3), (4, 5), (6, 7)), ((0, 1), (3, 2), (5, 4), (6, 7)),
        ((0, 1), (2, 3), (4, 5), (6, 7)), ((0, 7), (2, 1), (3, 4), (5, 6)),
        ((0, 1), (2, 3), (4, 5), (6, 7)), ((0, 1), (2, 3), (5, 4), (7, 6)),
    ),
)


LEAD = (((0, 5),), ((0, 6), (5, 2)), ((0, 7), (6, 3), (5, 4), (2, 1)))


def along_z(x, moves):
    pairs = [(16 * r + 2 * a + h, 16 * r + 2 * b + h) for r in range(16) for a, b in moves(r // 2) for h in range(2)]
    return lax.ppermute(x, ("row", "col"), pairs)


def per_device(a):
    r = lax.axis_index("row").astype(jnp.int32)
    c = lax.axis_index("col").astype(jnp.int32)
    pos = jnp.stack([r, c])
    swap = [(i, i ^ 1) for i in range(16)]
    x = a[:, :NB]
    here = c < 2

    lead = lax.all_to_all(x[:NB].reshape(16, 16, NB), "row", 0, 0, tiled=True)[0:2].reshape(32, NB)
    lead = jnp.where(here, lead, 0.0)
    for moves in LEAD:
        lead += along_z(lead, lambda d: moves if d < 5 else [((8 - s) % 8, (8 - t) % 8) for s, t in moves])
    panel = jnp.where(here, x, 0.0)
    panel += along_z(panel, lambda d: TREE[0][d])
    lead, panel, pos = lax.optimization_barrier((lead, panel, pos))

    pieces = panel.reshape(4, 16, 16, NB).transpose(1, 0, 2, 3).reshape(16, 64, NB)
    pieces = jnp.concatenate([pieces, jnp.broadcast_to(lead[None], (16, 32, NB))], axis=1)
    held = lax.all_to_all(pieces, "row", 0, 0, tiled=True)
    arrived = along_z(panel, lambda d: TREE[1][d])
    held, arrived, pos = lax.optimization_barrier((held, arrived, meanwhile(pos)))
    panel += arrived

    lead = held[:, 64:].reshape(16, 2, 16, NB)
    theirs = lax.ppermute(lead, "col", swap)
    mine = lax.dynamic_index_in_dim(held, c, 0, keepdims=False)[:64]
    other = lax.ppermute(lax.dynamic_index_in_dim(held, c ^ 1, 0, keepdims=False)[:64], "col", swap)
    mine, other, lead, theirs, panel = lax.optimization_barrier((mine, other, lead, theirs, panel))
    gc = jnp.stack([mine, other]).reshape(2, 4, 16, NB)
    gc = lax.all_to_all(jnp.broadcast_to(gc[None], (16, 2, 4, 16, NB)), "row", 0, 0, tiled=True)
    arrived = along_z(panel, lambda d: TREE[2][d])
    *factors, arrived = lax.optimization_barrier((*factor(pos, lead, theirs), arrived))
    panel += arrived
    p, q = solve_rows(pos, panel, lax.ppermute(panel, "col", swap), factors)
    a, p, q = (pltpu.with_memory_space_constraint(v, pltpu.HBM) for v in (a, p, q))
    return update(pos, a, p, q, gc)


def solution(mesh):
    return jax.shard_map(
        per_device,
        mesh=mesh,
        in_specs=(P("row", "col"),),
        out_specs=P("row", "col"),
        check_vma=False,
    )
```

```python
import jax
import jax.numpy as jnp
from jax import lax
from jax.experimental import pallas as pl
from jax.experimental.pallas import tpu as pltpu
from jax.sharding import PartitionSpec as P

NB = 256
HB = 128
STEP = 16
HIGH = lax.Precision.HIGHEST
F32 = jnp.float32
BF16 = jnp.bfloat16
VMEM = pl.BlockSpec(memory_space=pltpu.VMEM)
SMEM = pl.BlockSpec(memory_space=pltpu.SMEM)


def dot_nt(a, b):
    return lax.dot_general(a, b, (((1,), (1,)), ((), ())), precision=HIGH, preferred_element_type=F32)


def dot_nn(a, b):
    return lax.dot_general(a, b, (((1,), (0,)), ((), ())), precision=HIGH, preferred_element_type=F32)


def dot_tn(a, b):
    return lax.dot_general(a, b, (((0,), (0,)), ((), ())), precision=HIGH, preferred_element_type=F32)


def dot_nt_16(a, b):
    return lax.dot_general(a, b, (((1,), (1,)), ((), ())), preferred_element_type=F32)


def split3(x):
    hi = x.astype(BF16).astype(F32)
    rest = x - hi
    mid = rest.astype(BF16).astype(F32)
    return hi, mid, rest - mid


def dot_tn_short(a, b):
    ah, am, al = split3(a)
    bh, bm, bl = split3(b)
    left = jnp.concatenate([ah, ah, am, ah, al, am], axis=0).astype(BF16)
    right = jnp.concatenate([bh, bm, bh, bl, bh, bm], axis=0).astype(BF16)
    return lax.dot_general(left, right, (((0,), (0,)), ((), ())), preferred_element_type=F32)


def reciprocal(x):
    r = pl.reciprocal(x, approx=True)
    return r * (2.0 - x * r)


def inverse_root(x):
    r = lax.rsqrt(x)
    return r * (1.5 - 0.5 * x * r * r)


def factor_half(m_ref):
    sub = lax.broadcasted_iota(jnp.int32, (STEP, HB), 0)
    lane = lax.broadcasted_iota(jnp.int32, (STEP, HB), 1)
    odd = (sub & 1) == 1

    def spread(x, i):
        return jnp.broadcast_to(x[i:i + 1, :], (STEP, HB))

    for lo in range(0, HB, STEP):
        s = m_ref[lo:lo + STEP, :HB]
        v = m_ref[lo:lo + STEP, HB:]
        cols = [jnp.broadcast_to(s[:, lo + j:lo + j + 1], (STEP, HB)) for j in range(STEP)]
        first = jnp.ones((STEP, HB), F32)
        dets = first
        cross = first
        for j in range(0, STEP, 2):
            a, b, c = spread(cols[j], j), spread(cols[j], j + 1), spread(cols[j + 1], j + 1)
            det = a * c - b * b
            pair = (sub == j) | (sub == j + 1)
            first = jnp.where(pair, a, first)
            dets = jnp.where(pair, det, dets)
            cross = jnp.where(pair, b, cross)
            if j < STEP - 2:
                r = reciprocal(det)
                below = sub > j + 1
                f0 = jnp.where(below, (cols[j] * c - cols[j + 1] * b) * r, 0.0)
                f1 = jnp.where(below, (cols[j + 1] * a - cols[j] * b) * r, 0.0)
                for i in range(j + 2, STEP):
                    cols[i] = cols[i] - (f0 * spread(cols[i], j) + f1 * spread(cols[i], j + 1))
                s = s - (f0 * spread(s, j) + f1 * spread(s, j + 1))
                v = v - (f0 * spread(v, j) + f1 * spread(v, j + 1))
        ra = inverse_root(first)
        scale = jnp.where(odd, first * ra * inverse_root(dets), ra)
        mult = jnp.where(odd, cross * ra * ra, 0.0)
        s = jnp.where(lane >= lo + sub, (s - mult * pltpu.roll(s, 1, 0)) * scale, 0.0)
        v = (v - mult * pltpu.roll(v, 1, 0)) * scale
        uw = jnp.concatenate([s, v], axis=1)
        m_ref[lo:lo + STEP, :] = uw
        if lo + STEP < HB:
            full = dot_tn_short(s, uw)
            m_ref[lo + STEP:, :] = m_ref[lo + STEP:, :] - full[lo + STEP:, :]


def factor_kernel(pos_ref, mine_ref, theirs_ref, l_ref, w_ref, a_ref, s_ref, m_ref):
    lane0 = pos_ref[1] % 2 == 0
    for k in range(16):
        at = slice(16 * k, 16 * k + 16)
        mine = mine_ref[k]
        theirs = theirs_ref[k]
        a_ref[0, at, :] = jnp.where(lane0, mine[0], theirs[0])
        a_ref[1, at, :] = jnp.where(lane0, mine[1], theirs[1])
        a_ref[2, at, :] = jnp.where(lane0, theirs[1], mine[1])
    a00 = a_ref[0]
    a11 = a_ref[2]
    s_ref[:NB, :NB] = (a00 + a00.T) * 0.5
    s_ref[:NB, NB:] = a_ref[1].T
    s_ref[NB:, NB:] = (a11 + a11.T) * 0.5
    eye = (lax.broadcasted_iota(jnp.int32, (HB, HB), 0) == lax.broadcasted_iota(jnp.int32, (HB, HB), 1)).astype(F32)
    l_ref[...] = jnp.zeros((2 * NB, 2 * NB), F32)
    w_ref[...] = jnp.zeros((2 * NB, 2 * NB), F32)
    for k in range(4):
        lo = k * HB
        hi = lo + HB
        m_ref[:, :HB] = s_ref[lo:hi, lo:hi]
        m_ref[:, HB:] = eye
        factor_half(m_ref)
        w = m_ref[:, HB:]
        l_ref[lo:hi, lo:hi] = m_ref[:, :HB].T
        w_ref[lo:hi, lo:hi] = w
        if k < 3:
            row = dot_nn(w, s_ref[lo:hi, hi:])
            s_ref[lo:hi, hi:] = row
            s_ref[hi:, hi:] = s_ref[hi:, hi:] - dot_tn(row, row)
            l_ref[hi:, lo:hi] = row.T
        if k % 2 == 1:
            w_ref[lo:hi, lo - HB:lo] = -dot_nn(w, dot_nn(l_ref[lo:hi, lo - HB:lo], w_ref[lo - HB:lo, lo - HB:lo]))
    w_ref[NB:, :NB] = -dot_nn(w_ref[NB:, NB:], dot_nn(l_ref[NB:, :NB], w_ref[:NB, :NB]))


def factor(pos, mine, theirs):
    both = jax.ShapeDtypeStruct((2 * NB, 2 * NB), F32)
    return pl.pallas_call(
        factor_kernel,
        out_shape=[both] * 2,
        in_specs=[SMEM, VMEM, VMEM],
        out_specs=[VMEM] * 2,
        scratch_shapes=[
            pltpu.VMEM((3, NB, NB), F32),
            pltpu.VMEM((2 * NB, 2 * NB), F32),
            pltpu.VMEM((HB, 2 * HB), F32),
        ],
        compiler_params=pltpu.CompilerParams(vmem_limit_bytes=16 * 2**20),
        cost_estimate=pl.CostEstimate(flops=15_000_000_000, bytes_accessed=4_000_000, transcendentals=0),
        name="factor_lead",
    )(pos, mine, theirs)


def meanwhile(pos):
    def kernel(x_ref, o_ref):
        o_ref[0] = x_ref[0]
        o_ref[1] = x_ref[1]

    return pl.pallas_call(
        kernel,
        out_shape=jax.ShapeDtypeStruct(pos.shape, pos.dtype),
        in_specs=[SMEM],
        out_specs=SMEM,
        cost_estimate=pl.CostEstimate(flops=40_000_000_000, bytes_accessed=100_000_000, transcendentals=0),
        name="meanwhile",
    )(pos)


def rows_kernel(pos_ref, mine_ref, other_ref, l_ref, w_ref, p_hbm, q_hbm, p_ref, q_ref, p_sem, q_sem):
    r = pos_ref[0]
    c = pos_ref[1]
    n = 2 * NB
    lane0 = c % 2 == 0
    copies = []
    for k in range(4):
        at = slice(k * NB, (k + 1) * NB)
        mine = mine_ref[at, :]
        other = other_ref[at, :]
        g0 = jnp.where(lane0, mine, other)
        g1 = jnp.where(lane0, other, mine)
        p0 = dot_nt(g0, w_ref[:NB, :NB])
        p1 = dot_nt(jnp.concatenate([g0, g1], axis=1), w_ref[NB:, :])
        q0 = dot_nn(jnp.concatenate([p0, p1], axis=1), w_ref[:, :NB])
        q1 = dot_nn(p1, w_ref[NB:, NB:])
        for h, part in enumerate(split3(jnp.concatenate([q0, q1], axis=1))):
            q_ref[at, h * n:(h + 1) * n] = part.astype(BF16)
        copies.append(pltpu.make_async_copy(q_ref.at[at], q_hbm.at[at], q_sem.at[k]))
        copies[-1].start()
        p = jnp.where(c == 0, p0, p1)
        if k == 0:
            zero = jnp.zeros((NB, NB), F32)
            p = jnp.where(r == 0, jnp.where(c == 0, l_ref[:NB, :NB], zero), p)
            p = jnp.where(r == 1, jnp.where(c == 0, l_ref[NB:, :NB], l_ref[NB:, NB:]), p)
        p_ref[at, :] = p
    @pl.when(c < 2)
    def _():
        copy = pltpu.make_async_copy(p_ref, p_hbm, p_sem)
        copy.start()
        copy.wait()

    for copy in copies:
        copy.wait()


def solve_rows(pos, mine, other, factors):
    hbm = pl.BlockSpec(memory_space=pltpu.HBM)
    p = jax.ShapeDtypeStruct((4 * NB, NB), F32)
    q = jax.ShapeDtypeStruct((4 * NB, 6 * NB), BF16)
    return pl.pallas_call(
        rows_kernel,
        out_shape=[pltpu.HBM(p.shape, F32), pltpu.HBM(q.shape, BF16)],
        in_specs=[SMEM] + [VMEM] * 4,
        out_specs=[hbm] * 2,
        scratch_shapes=[
            pltpu.VMEM(p.shape, F32),
            pltpu.VMEM(q.shape, BF16),
            pltpu.SemaphoreType.DMA(()),
            pltpu.SemaphoreType.DMA((4,)),
        ],
        compiler_params=pltpu.CompilerParams(vmem_limit_bytes=20 * 2**20),
        cost_estimate=pl.CostEstimate(flops=9_000_000_000, bytes_accessed=5_000_000, transcendentals=0),
        name="solve_rows",
    )(pos, mine, other, *factors)


def update_kernel(pos_ref, a_hbm, p_hbm, q_hbm, gc_ref, o_hbm, a_ref, q_ref, g_ref, o_ref, load_sems, store_sems, panel_sem):
    r = pos_ref[0]
    c = pos_ref[1]
    n = 2 * NB
    order = (3, 2, 1, 0)
    part = [slice(k * NB, (k + 1) * NB) for k in range(4)]
    loads = {
        k: [
            pltpu.make_async_copy(q_hbm.at[part[k]], q_ref.at[part[k]], load_sems.at[0, k]),
            pltpu.make_async_copy(a_hbm.at[part[k]], a_ref.at[part[k]], load_sems.at[1, k]),
        ]
        for k in order
    }
    for k in order:
        for copy in loads[k]:
            copy.start()
    panel = pltpu.make_async_copy(p_hbm, o_ref.at[:, :NB], panel_sem)

    @pl.when(c < 2)
    def _():
        panel.start()

    def block(k, m):
        small = dot_nt_16(q_ref[part[k], :], g_ref[part[m], :])
        small += dot_nt_16(q_ref[part[k], :2 * n], g_ref[part[m], n:])
        main = dot_nt_16(q_ref[part[k], :n], g_ref[part[m], 2 * n:])
        o_ref[part[k], part[m]] = a_ref[part[k], part[m]] - (small + main)

    def clear(k, m):
        o_ref[part[k], part[m]] = jnp.zeros((NB, NB), F32)

    core = c % 2
    for m in range(4):
        for h, lane in enumerate((core, 1 - core)):
            hi, mid, lo = split3(gc_ref[:, lane, m].reshape(NB, NB))
            for k, piece in enumerate((lo, mid, hi)):
                g_ref[part[m], k * n + h * NB:k * n + (h + 1) * NB] = piece.astype(BF16)
        for k in range(m):
            clear(k, m)

    stores = []
    for k in order:
        for copy in loads[k]:
            copy.wait()
        for m in range(1, k):
            block(k, m)

        @pl.when(c >= 2)
        def _():
            if k > 0:
                block(k, 0)

        if k == 3:
            @pl.when(c < 2)
            def _():
                panel.wait()

        inside = r >= c if k > 0 else (r >= c) & (c >= 2)
        outside = r < c if k > 0 else (r < c) & (c >= 2)

        @pl.when(inside)
        def _():
            block(k, k)

        @pl.when(outside)
        def _():
            clear(k, k)

        stores.append(pltpu.make_async_copy(o_ref.at[part[k]], o_hbm.at[part[k]], store_sems.at[k]))
        stores[-1].start()
    for copy in stores:
        copy.wait()


def update(pos, a, p, q, gc):
    hbm = pl.BlockSpec(memory_space=pltpu.HBM)
    return pl.pallas_call(
        update_kernel,
        out_shape=jax.ShapeDtypeStruct(a.shape, F32),
        in_specs=[SMEM, hbm, hbm, hbm, VMEM],
        out_specs=hbm,
        scratch_shapes=[
            pltpu.VMEM(a.shape, F32),
            pltpu.VMEM(q.shape, BF16),
            pltpu.VMEM(q.shape, BF16),
            pltpu.VMEM(a.shape, F32),
            pltpu.SemaphoreType.DMA((2, 4)),
            pltpu.SemaphoreType.DMA((4,)),
            pltpu.SemaphoreType.DMA(()),
        ],
        compiler_params=pltpu.CompilerParams(vmem_limit_bytes=32 * 2**20),
        cost_estimate=pl.CostEstimate(flops=8_000_000_000, bytes_accessed=13_000_000, transcendentals=0),
        name="update",
    )(pos, a, p, q, gc)


TREE = (
    tuple(((0, d or 4),) for d in range(8)),
    (
        ((0, 6), (4, 2)), ((0, 6), (1, 3)), ((0, 6), (2, 4)), ((0, 6), (3, 5)),
        ((0, 2), (4, 6)), ((0, 2), (5, 3)), ((0, 2), (6, 4)), ((0, 2), (7, 5)),
    ),
    (
        ((0, 7), (6, 5), (4, 3), (2, 1)), ((0, 7), (1, 2), (3, 4), (6, 5)),
        ((0, 1), (2, 3), (4, 5), (6, 7)), ((0, 1), (3, 2), (5, 4), (6, 7)),
        ((0, 1), (2, 3), (4, 5), (6, 7)), ((0, 7), (2, 1), (3, 4), (5, 6)),
        ((0, 1), (2, 3), (4, 5), (6, 7)), ((0, 1), (2, 3), (5, 4), (7, 6)),
    ),
)


LEAD = (((0, 5),), ((0, 7), (5, 3)), ((0, 1), (7, 6), (5, 4), (3, 2)))


def along_z(x, moves):
    pairs = [(16 * r + 2 * a + h, 16 * r + 2 * b + h) for r in range(16) for a, b in moves(r // 2) for h in range(2)]
    return lax.ppermute(x, ("row", "col"), pairs)


def per_device(a):
    r = lax.axis_index("row").astype(jnp.int32)
    c = lax.axis_index("col").astype(jnp.int32)
    pos = jnp.stack([r, c])
    swap = [(i, i ^ 1) for i in range(16)]
    x = a[:, :NB]
    here = c < 2

    lead = lax.all_to_all(x[:NB].reshape(16, 16, NB), "row", 0, 0, tiled=True)[0:2].reshape(32, NB)
    lead = jnp.where(here, lead, 0.0)
    for moves in LEAD:
        lead += along_z(lead, lambda d: moves if d < 5 else [((8 - s) % 8, (8 - t) % 8) for s, t in moves])
    panel = jnp.where(here, x, 0.0)
    panel += along_z(panel, lambda d: TREE[0][d])
    lead, panel, pos = lax.optimization_barrier((lead, panel, pos))

    pieces = panel.reshape(4, 16, 16, NB).transpose(1, 0, 2, 3).reshape(16, 64, NB)
    pieces = jnp.concatenate([pieces, jnp.broadcast_to(lead[None], (16, 32, NB))], axis=1)
    held = lax.all_to_all(pieces, "row", 0, 0, tiled=True)
    arrived = along_z(panel, lambda d: TREE[1][d])
    held, arrived, pos = lax.optimization_barrier((held, arrived, meanwhile(pos)))
    panel += arrived

    lead = held[:, 64:].reshape(16, 2, 16, NB)
    theirs = lax.ppermute(lead, "col", swap)
    mine = lax.dynamic_index_in_dim(held, c, 0, keepdims=False)[:64]
    other = lax.ppermute(lax.dynamic_index_in_dim(held, c ^ 1, 0, keepdims=False)[:64], "col", swap)
    mine, other, lead, theirs, panel = lax.optimization_barrier((mine, other, lead, theirs, panel))
    gc = jnp.stack([mine, other]).reshape(2, 4, 16, NB)
    gc = lax.all_to_all(jnp.broadcast_to(gc[None], (16, 2, 4, 16, NB)), "row", 0, 0, tiled=True)
    arrived = along_z(panel, lambda d: TREE[2][d])
    *factors, arrived = lax.optimization_barrier((*factor(pos, lead, theirs), arrived))
    panel += arrived
    p, q = solve_rows(pos, panel, lax.ppermute(panel, "col", swap), factors)
    a, p, q = (pltpu.with_memory_space_constraint(v, pltpu.HBM) for v in (a, p, q))
    return update(pos, a, p, q, gc)


def solution(mesh):
    return jax.shard_map(
        per_device,
        mesh=mesh,
        in_specs=(P("row", "col"),),
        out_specs=P("row", "col"),
        check_vma=False,
    )
```

```python
import jax
import jax.numpy as jnp
from jax import lax
from jax.experimental import pallas as pl
from jax.experimental.pallas import tpu as pltpu
from jax.sharding import PartitionSpec as P

NB = 256
HB = 128
STEP = 16
HIGH = lax.Precision.HIGHEST
F32 = jnp.float32
BF16 = jnp.bfloat16
VMEM = pl.BlockSpec(memory_space=pltpu.VMEM)
SMEM = pl.BlockSpec(memory_space=pltpu.SMEM)


def dot_nt(a, b):
    return lax.dot_general(a, b, (((1,), (1,)), ((), ())), precision=HIGH, preferred_element_type=F32)


def dot_nn(a, b):
    return lax.dot_general(a, b, (((1,), (0,)), ((), ())), precision=HIGH, preferred_element_type=F32)


def dot_tn(a, b):
    return lax.dot_general(a, b, (((0,), (0,)), ((), ())), precision=HIGH, preferred_element_type=F32)


def dot_nt_16(a, b):
    return lax.dot_general(a, b, (((1,), (1,)), ((), ())), preferred_element_type=F32)


def split3(x):
    hi = x.astype(BF16).astype(F32)
    rest = x - hi
    mid = rest.astype(BF16).astype(F32)
    return hi, mid, rest - mid


def dot_tn_short(a, b):
    ah, am, al = split3(a)
    bh, bm, bl = split3(b)
    left = jnp.concatenate([ah, ah, am, ah, al, am], axis=0).astype(BF16)
    right = jnp.concatenate([bh, bm, bh, bl, bh, bm], axis=0).astype(BF16)
    return lax.dot_general(left, right, (((0,), (0,)), ((), ())), preferred_element_type=F32)


def reciprocal(x):
    r = pl.reciprocal(x, approx=True)
    return r * (2.0 - x * r)


def inverse_root(x):
    r = lax.rsqrt(x)
    return r * (1.5 - 0.5 * x * r * r)


def factor_half(m_ref):
    sub = lax.broadcasted_iota(jnp.int32, (STEP, HB), 0)
    lane = lax.broadcasted_iota(jnp.int32, (STEP, HB), 1)
    odd = (sub & 1) == 1

    def spread(x, i):
        return jnp.broadcast_to(x[i:i + 1, :], (STEP, HB))

    for lo in range(0, HB, STEP):
        s = m_ref[lo:lo + STEP, :HB]
        v = m_ref[lo:lo + STEP, HB:]
        cols = [jnp.broadcast_to(s[:, lo + j:lo + j + 1], (STEP, HB)) for j in range(STEP)]
        first = jnp.ones((STEP, HB), F32)
        dets = first
        cross = first
        for j in range(0, STEP, 2):
            a, b, c = spread(cols[j], j), spread(cols[j], j + 1), spread(cols[j + 1], j + 1)
            det = a * c - b * b
            pair = (sub == j) | (sub == j + 1)
            first = jnp.where(pair, a, first)
            dets = jnp.where(pair, det, dets)
            cross = jnp.where(pair, b, cross)
            if j < STEP - 2:
                r = reciprocal(det)
                below = sub > j + 1
                f0 = jnp.where(below, (cols[j] * c - cols[j + 1] * b) * r, 0.0)
                f1 = jnp.where(below, (cols[j + 1] * a - cols[j] * b) * r, 0.0)
                for i in range(j + 2, STEP):
                    cols[i] = cols[i] - (f0 * spread(cols[i], j) + f1 * spread(cols[i], j + 1))
                s = s - (f0 * spread(s, j) + f1 * spread(s, j + 1))
                v = v - (f0 * spread(v, j) + f1 * spread(v, j + 1))
        ra = inverse_root(first)
        scale = jnp.where(odd, first * ra * inverse_root(dets), ra)
        mult = jnp.where(odd, cross * ra * ra, 0.0)
        s = jnp.where(lane >= lo + sub, (s - mult * pltpu.roll(s, 1, 0)) * scale, 0.0)
        v = (v - mult * pltpu.roll(v, 1, 0)) * scale
        uw = jnp.concatenate([s, v], axis=1)
        m_ref[lo:lo + STEP, :] = uw
        if lo + STEP < HB:
            full = dot_tn_short(s, uw)
            m_ref[lo + STEP:, :] = m_ref[lo + STEP:, :] - full[lo + STEP:, :]


def factor_kernel(pos_ref, mine_ref, theirs_ref, l_ref, w_ref, a_ref, s_ref, m_ref):
    lane0 = pos_ref[1] % 2 == 0
    for k in range(16):
        at = slice(16 * k, 16 * k + 16)
        mine = mine_ref[k]
        theirs = theirs_ref[k]
        a_ref[0, at, :] = jnp.where(lane0, mine[0], theirs[0])
        a_ref[1, at, :] = jnp.where(lane0, mine[1], theirs[1])
        a_ref[2, at, :] = jnp.where(lane0, theirs[1], mine[1])
    a00 = a_ref[0]
    a11 = a_ref[2]
    s_ref[:NB, :NB] = (a00 + a00.T) * 0.5
    s_ref[:NB, NB:] = a_ref[1].T
    s_ref[NB:, NB:] = (a11 + a11.T) * 0.5
    eye = (lax.broadcasted_iota(jnp.int32, (HB, HB), 0) == lax.broadcasted_iota(jnp.int32, (HB, HB), 1)).astype(F32)
    l_ref[...] = jnp.zeros((2 * NB, 2 * NB), F32)
    w_ref[...] = jnp.zeros((2 * NB, 2 * NB), F32)
    for k in range(4):
        lo = k * HB
        hi = lo + HB
        m_ref[:, :HB] = s_ref[lo:hi, lo:hi]
        m_ref[:, HB:] = eye
        factor_half(m_ref)
        w = m_ref[:, HB:]
        l_ref[lo:hi, lo:hi] = m_ref[:, :HB].T
        w_ref[lo:hi, lo:hi] = w
        if k < 3:
            row = dot_nn(w, s_ref[lo:hi, hi:])
            s_ref[lo:hi, hi:] = row
            s_ref[hi:, hi:] = s_ref[hi:, hi:] - dot_tn(row, row)
            l_ref[hi:, lo:hi] = row.T
        if k % 2 == 1:
            w_ref[lo:hi, lo - HB:lo] = -dot_nn(w, dot_nn(l_ref[lo:hi, lo - HB:lo], w_ref[lo - HB:lo, lo - HB:lo]))
    w_ref[NB:, :NB] = -dot_nn(w_ref[NB:, NB:], dot_nn(l_ref[NB:, :NB], w_ref[:NB, :NB]))


def factor(pos, mine, theirs):
    both = jax.ShapeDtypeStruct((2 * NB, 2 * NB), F32)
    return pl.pallas_call(
        factor_kernel,
        out_shape=[both] * 2,
        in_specs=[SMEM, VMEM, VMEM],
        out_specs=[VMEM] * 2,
        scratch_shapes=[
            pltpu.VMEM((3, NB, NB), F32),
            pltpu.VMEM((2 * NB, 2 * NB), F32),
            pltpu.VMEM((HB, 2 * HB), F32),
        ],
        compiler_params=pltpu.CompilerParams(vmem_limit_bytes=16 * 2**20),
        cost_estimate=pl.CostEstimate(flops=1_000_000, bytes_accessed=4_000_000, transcendentals=0),
        name="factor_lead",
    )(pos, mine, theirs)


def meanwhile(pos):
    def kernel(x_ref, o_ref):
        o_ref[0] = x_ref[0]
        o_ref[1] = x_ref[1]

    return pl.pallas_call(
        kernel,
        out_shape=jax.ShapeDtypeStruct(pos.shape, pos.dtype),
        in_specs=[SMEM],
        out_specs=SMEM,
        cost_estimate=pl.CostEstimate(flops=40_000_000_000, bytes_accessed=100_000_000, transcendentals=0),
        name="meanwhile",
    )(pos)


def rows_kernel(pos_ref, mine_ref, other_ref, l_ref, w_ref, p_hbm, q_hbm, p_ref, q_ref, p_sem, q_sem):
    r = pos_ref[0]
    c = pos_ref[1]
    n = 2 * NB
    lane0 = c % 2 == 0
    copies = []
    for k in range(4):
        at = slice(k * NB, (k + 1) * NB)
        mine = mine_ref[at, :]
        other = other_ref[at, :]
        g0 = jnp.where(lane0, mine, other)
        g1 = jnp.where(lane0, other, mine)
        p0 = dot_nt(g0, w_ref[:NB, :NB])
        p1 = dot_nt(jnp.concatenate([g0, g1], axis=1), w_ref[NB:, :])
        q0 = dot_nn(jnp.concatenate([p0, p1], axis=1), w_ref[:, :NB])
        q1 = dot_nn(p1, w_ref[NB:, NB:])
        for h, part in enumerate(split3(jnp.concatenate([q0, q1], axis=1))):
            q_ref[at, h * n:(h + 1) * n] = part.astype(BF16)
        copies.append(pltpu.make_async_copy(q_ref.at[at], q_hbm.at[at], q_sem.at[k]))
        copies[-1].start()
        p = jnp.where(c == 0, p0, p1)
        if k == 0:
            zero = jnp.zeros((NB, NB), F32)
            p = jnp.where(r == 0, jnp.where(c == 0, l_ref[:NB, :NB], zero), p)
            p = jnp.where(r == 1, jnp.where(c == 0, l_ref[NB:, :NB], l_ref[NB:, NB:]), p)
        p_ref[at, :] = p
    @pl.when(c < 2)
    def _():
        copy = pltpu.make_async_copy(p_ref, p_hbm, p_sem)
        copy.start()
        copy.wait()

    for copy in copies:
        copy.wait()


def solve_rows(pos, mine, other, factors):
    hbm = pl.BlockSpec(memory_space=pltpu.HBM)
    p = jax.ShapeDtypeStruct((4 * NB, NB), F32)
    q = jax.ShapeDtypeStruct((4 * NB, 6 * NB), BF16)
    return pl.pallas_call(
        rows_kernel,
        out_shape=[pltpu.HBM(p.shape, F32), pltpu.HBM(q.shape, BF16)],
        in_specs=[SMEM] + [VMEM] * 4,
        out_specs=[hbm] * 2,
        scratch_shapes=[
            pltpu.VMEM(p.shape, F32),
            pltpu.VMEM(q.shape, BF16),
            pltpu.SemaphoreType.DMA(()),
            pltpu.SemaphoreType.DMA((4,)),
        ],
        compiler_params=pltpu.CompilerParams(vmem_limit_bytes=20 * 2**20),
        cost_estimate=pl.CostEstimate(flops=1_000_000, bytes_accessed=5_000_000, transcendentals=0),
        name="solve_rows",
    )(pos, mine, other, *factors)


def update_kernel(pos_ref, a_hbm, p_hbm, q_hbm, gc_ref, o_hbm, a_ref, q_ref, g_ref, o_ref, load_sems, store_sems, panel_sem):
    r = pos_ref[0]
    c = pos_ref[1]
    n = 2 * NB
    order = (3, 2, 1, 0)
    part = [slice(k * NB, (k + 1) * NB) for k in range(4)]
    loads = {
        k: [
            pltpu.make_async_copy(q_hbm.at[part[k]], q_ref.at[part[k]], load_sems.at[0, k]),
            pltpu.make_async_copy(a_hbm.at[part[k]], a_ref.at[part[k]], load_sems.at[1, k]),
        ]
        for k in order
    }
    for k in order:
        for copy in loads[k]:
            copy.start()
    panel = pltpu.make_async_copy(p_hbm, o_ref.at[:, :NB], panel_sem)

    @pl.when(c < 2)
    def _():
        panel.start()

    def block(k, m):
        small = dot_nt_16(q_ref[part[k], :], g_ref[part[m], :])
        small += dot_nt_16(q_ref[part[k], :2 * n], g_ref[part[m], n:])
        main = dot_nt_16(q_ref[part[k], :n], g_ref[part[m], 2 * n:])
        o_ref[part[k], part[m]] = a_ref[part[k], part[m]] - (small + main)

    def clear(k, m):
        o_ref[part[k], part[m]] = jnp.zeros((NB, NB), F32)

    core = c % 2
    for m in range(4):
        for h, lane in enumerate((core, 1 - core)):
            hi, mid, lo = split3(gc_ref[:, lane, m].reshape(NB, NB))
            for k, piece in enumerate((lo, mid, hi)):
                g_ref[part[m], k * n + h * NB:k * n + (h + 1) * NB] = piece.astype(BF16)
        for k in range(m):
            clear(k, m)

    stores = []
    for k in order:
        for copy in loads[k]:
            copy.wait()
        for m in range(1, k):
            block(k, m)

        @pl.when(c >= 2)
        def _():
            if k > 0:
                block(k, 0)

        if k == 3:
            @pl.when(c < 2)
            def _():
                panel.wait()

        inside = r >= c if k > 0 else (r >= c) & (c >= 2)
        outside = r < c if k > 0 else (r < c) & (c >= 2)

        @pl.when(inside)
        def _():
            block(k, k)

        @pl.when(outside)
        def _():
            clear(k, k)

        stores.append(pltpu.make_async_copy(o_ref.at[part[k]], o_hbm.at[part[k]], store_sems.at[k]))
        stores[-1].start()
    for copy in stores:
        copy.wait()


def update(pos, a, p, q, gc):
    hbm = pl.BlockSpec(memory_space=pltpu.HBM)
    return pl.pallas_call(
        update_kernel,
        out_shape=jax.ShapeDtypeStruct(a.shape, F32),
        in_specs=[SMEM, hbm, hbm, hbm, VMEM],
        out_specs=hbm,
        scratch_shapes=[
            pltpu.VMEM(a.shape, F32),
            pltpu.VMEM(q.shape, BF16),
            pltpu.VMEM(q.shape, BF16),
            pltpu.VMEM(a.shape, F32),
            pltpu.SemaphoreType.DMA((2, 4)),
            pltpu.SemaphoreType.DMA((4,)),
            pltpu.SemaphoreType.DMA(()),
        ],
        compiler_params=pltpu.CompilerParams(vmem_limit_bytes=32 * 2**20),
        cost_estimate=pl.CostEstimate(flops=8_000_000_000, bytes_accessed=13_000_000, transcendentals=0),
        name="update",
    )(pos, a, p, q, gc)


TREE = (
    tuple(((0, d or 4),) for d in range(8)),
    (
        ((0, 6), (4, 2)), ((0, 6), (1, 3)), ((0, 6), (2, 4)), ((0, 6), (3, 5)),
        ((0, 2), (4, 6)), ((0, 2), (5, 3)), ((0, 2), (6, 4)), ((0, 2), (7, 5)),
    ),
    (
        ((0, 7), (6, 5), (4, 3), (2, 1)), ((0, 7), (1, 2), (3, 4), (6, 5)),
        ((0, 1), (2, 3), (4, 5), (6, 7)), ((0, 1), (3, 2), (5, 4), (6, 7)),
        ((0, 1), (2, 3), (4, 5), (6, 7)), ((0, 7), (2, 1), (3, 4), (5, 6)),
        ((0, 1), (2, 3), (4, 5), (6, 7)), ((0, 1), (2, 3), (5, 4), (7, 6)),
    ),
)


LEAD = (((0, 5),), ((0, 7), (5, 3)), ((0, 1), (7, 6), (5, 4), (3, 2)))


def along_z(x, moves):
    pairs = [(16 * r + 2 * a + h, 16 * r + 2 * b + h) for r in range(16) for a, b in moves(r // 2) for h in range(2)]
    return lax.ppermute(x, ("row", "col"), pairs)


def per_device(a):
    r = lax.axis_index("row").astype(jnp.int32)
    c = lax.axis_index("col").astype(jnp.int32)
    pos = jnp.stack([r, c])
    swap = [(i, i ^ 1) for i in range(16)]
    x = a[:, :NB]
    here = c < 2

    lead = lax.all_to_all(x[:NB].reshape(16, 16, NB), "row", 0, 0, tiled=True)[0:2].reshape(32, NB)
    lead = jnp.where(here, lead, 0.0)
    for moves in LEAD:
        lead += along_z(lead, lambda d: moves if d < 5 else [((8 - s) % 8, (8 - t) % 8) for s, t in moves])
    panel = jnp.where(here, x, 0.0)
    panel += along_z(panel, lambda d: TREE[0][d])
    lead, panel, pos = lax.optimization_barrier((lead, panel, pos))

    pieces = panel.reshape(4, 16, 16, NB).transpose(1, 0, 2, 3).reshape(16, 64, NB)
    pieces = jnp.concatenate([pieces, jnp.broadcast_to(lead[None], (16, 32, NB))], axis=1)
    held = lax.all_to_all(pieces, "row", 0, 0, tiled=True)
    arrived, pos = lax.optimization_barrier((along_z(panel, lambda d: TREE[1][d]), meanwhile(pos)))
    panel += arrived
    arrived = along_z(panel, lambda d: TREE[2][d])
    held, panel, pos = lax.optimization_barrier((held, panel, pos))

    lead = held[:, 64:].reshape(16, 2, 16, NB)
    theirs = lax.ppermute(lead, "col", swap)
    mine = lax.dynamic_index_in_dim(held, c, 0, keepdims=False)[:64]
    other = lax.ppermute(lax.dynamic_index_in_dim(held, c ^ 1, 0, keepdims=False)[:64], "col", swap)
    mine, other, lead, theirs, panel = lax.optimization_barrier((mine, other, lead, theirs, panel))
    gc = jnp.stack([mine, other]).reshape(2, 4, 16, NB)
    gc = lax.all_to_all(jnp.broadcast_to(gc[None], (16, 2, 4, 16, NB)), "row", 0, 0, tiled=True)
    *factors, arrived = lax.optimization_barrier((*factor(pos, lead, theirs), arrived))
    panel += arrived
    p, q = solve_rows(pos, panel, lax.ppermute(panel, "col", swap), factors)
    a, p, q = (pltpu.with_memory_space_constraint(v, pltpu.HBM) for v in (a, p, q))
    return update(pos, a, p, q, gc)


def solution(mesh):
    return jax.shard_map(
        per_device,
        mesh=mesh,
        in_specs=(P("row", "col"),),
        out_specs=P("row", "col"),
        check_vma=False,
    )
```

```python
import jax
import jax.numpy as jnp
from jax import lax
from jax.experimental import pallas as pl
from jax.experimental.pallas import tpu as pltpu
from jax.sharding import PartitionSpec as P

NB = 256
HB = 128
STEP = 16
HIGH = lax.Precision.HIGHEST
F32 = jnp.float32
BF16 = jnp.bfloat16
VMEM = pl.BlockSpec(memory_space=pltpu.VMEM)
SMEM = pl.BlockSpec(memory_space=pltpu.SMEM)


def dot_nt(a, b):
    return lax.dot_general(a, b, (((1,), (1,)), ((), ())), precision=HIGH, preferred_element_type=F32)


def dot_nn(a, b):
    return lax.dot_general(a, b, (((1,), (0,)), ((), ())), precision=HIGH, preferred_element_type=F32)


def dot_tn(a, b):
    return lax.dot_general(a, b, (((0,), (0,)), ((), ())), precision=HIGH, preferred_element_type=F32)


def dot_nt_16(a, b):
    return lax.dot_general(a, b, (((1,), (1,)), ((), ())), preferred_element_type=F32)


def split3(x):
    hi = x.astype(BF16).astype(F32)
    rest = x - hi
    mid = rest.astype(BF16).astype(F32)
    return hi, mid, rest - mid


def dot_tn_short(a, b):
    ah, am, al = split3(a)
    bh, bm, bl = split3(b)
    left = jnp.concatenate([ah, ah, am, ah, al, am], axis=0).astype(BF16)
    right = jnp.concatenate([bh, bm, bh, bl, bh, bm], axis=0).astype(BF16)
    return lax.dot_general(left, right, (((0,), (0,)), ((), ())), preferred_element_type=F32)


def reciprocal(x):
    r = pl.reciprocal(x, approx=True)
    return r * (2.0 - x * r)


def inverse_root(x):
    r = lax.rsqrt(x)
    return r * (1.5 - 0.5 * x * r * r)


def factor_half(m_ref):
    sub = lax.broadcasted_iota(jnp.int32, (STEP, HB), 0)
    lane = lax.broadcasted_iota(jnp.int32, (STEP, HB), 1)
    odd = (sub & 1) == 1

    def spread(x, i):
        return jnp.broadcast_to(x[i:i + 1, :], (STEP, HB))

    for lo in range(0, HB, STEP):
        s = m_ref[lo:lo + STEP, :HB]
        v = m_ref[lo:lo + STEP, HB:]
        cols = [jnp.broadcast_to(s[:, lo + j:lo + j + 1], (STEP, HB)) for j in range(STEP)]
        first = jnp.ones((STEP, HB), F32)
        dets = first
        cross = first
        for j in range(0, STEP, 2):
            a, b, c = spread(cols[j], j), spread(cols[j], j + 1), spread(cols[j + 1], j + 1)
            det = a * c - b * b
            pair = (sub == j) | (sub == j + 1)
            first = jnp.where(pair, a, first)
            dets = jnp.where(pair, det, dets)
            cross = jnp.where(pair, b, cross)
            if j < STEP - 2:
                r = reciprocal(det)
                below = sub > j + 1
                f0 = jnp.where(below, (cols[j] * c - cols[j + 1] * b) * r, 0.0)
                f1 = jnp.where(below, (cols[j + 1] * a - cols[j] * b) * r, 0.0)
                for i in range(j + 2, STEP):
                    cols[i] = cols[i] - (f0 * spread(cols[i], j) + f1 * spread(cols[i], j + 1))
                s = s - (f0 * spread(s, j) + f1 * spread(s, j + 1))
                v = v - (f0 * spread(v, j) + f1 * spread(v, j + 1))
        ra = inverse_root(first)
        scale = jnp.where(odd, first * ra * inverse_root(dets), ra)
        mult = jnp.where(odd, cross * ra * ra, 0.0)
        s = jnp.where(lane >= lo + sub, (s - mult * pltpu.roll(s, 1, 0)) * scale, 0.0)
        v = (v - mult * pltpu.roll(v, 1, 0)) * scale
        uw = jnp.concatenate([s, v], axis=1)
        m_ref[lo:lo + STEP, :] = uw
        if lo + STEP < HB:
            full = dot_tn_short(s, uw)
            m_ref[lo + STEP:, :] = m_ref[lo + STEP:, :] - full[lo + STEP:, :]


def factor_kernel(pos_ref, mine_ref, theirs_ref, l_ref, w_ref, a_ref, s_ref, m_ref):
    lane0 = pos_ref[1] % 2 == 0
    for k in range(16):
        at = slice(16 * k, 16 * k + 16)
        mine = mine_ref[k]
        theirs = theirs_ref[k]
        a_ref[0, at, :] = jnp.where(lane0, mine[0], theirs[0])
        a_ref[1, at, :] = jnp.where(lane0, mine[1], theirs[1])
        a_ref[2, at, :] = jnp.where(lane0, theirs[1], mine[1])
    a00 = a_ref[0]
    a11 = a_ref[2]
    s_ref[:NB, :NB] = (a00 + a00.T) * 0.5
    s_ref[:NB, NB:] = a_ref[1].T
    s_ref[NB:, NB:] = (a11 + a11.T) * 0.5
    eye = (lax.broadcasted_iota(jnp.int32, (HB, HB), 0) == lax.broadcasted_iota(jnp.int32, (HB, HB), 1)).astype(F32)
    l_ref[...] = jnp.zeros((2 * NB, 2 * NB), F32)
    w_ref[...] = jnp.zeros((2 * NB, 2 * NB), F32)
    for k in range(4):
        lo = k * HB
        hi = lo + HB
        m_ref[:, :HB] = s_ref[lo:hi, lo:hi]
        m_ref[:, HB:] = eye
        factor_half(m_ref)
        w = m_ref[:, HB:]
        l_ref[lo:hi, lo:hi] = m_ref[:, :HB].T
        w_ref[lo:hi, lo:hi] = w
        if k < 3:
            row = dot_nn(w, s_ref[lo:hi, hi:])
            s_ref[lo:hi, hi:] = row
            s_ref[hi:, hi:] = s_ref[hi:, hi:] - dot_tn(row, row)
            l_ref[hi:, lo:hi] = row.T
        if k % 2 == 1:
            w_ref[lo:hi, lo - HB:lo] = -dot_nn(w, dot_nn(l_ref[lo:hi, lo - HB:lo], w_ref[lo - HB:lo, lo - HB:lo]))
    w_ref[NB:, :NB] = -dot_nn(w_ref[NB:, NB:], dot_nn(l_ref[NB:, :NB], w_ref[:NB, :NB]))


def factor(pos, mine, theirs):
    both = jax.ShapeDtypeStruct((2 * NB, 2 * NB), F32)
    return pl.pallas_call(
        factor_kernel,
        out_shape=[both] * 2,
        in_specs=[SMEM, VMEM, VMEM],
        out_specs=[VMEM] * 2,
        scratch_shapes=[
            pltpu.VMEM((3, NB, NB), F32),
            pltpu.VMEM((2 * NB, 2 * NB), F32),
            pltpu.VMEM((HB, 2 * HB), F32),
        ],
        compiler_params=pltpu.CompilerParams(vmem_limit_bytes=16 * 2**20),
        cost_estimate=pl.CostEstimate(flops=1_000_000, bytes_accessed=4_000_000, transcendentals=0),
        name="factor_lead",
    )(pos, mine, theirs)


def meanwhile(pos):
    def kernel(x_ref, o_ref):
        o_ref[0] = x_ref[0]
        o_ref[1] = x_ref[1]

    return pl.pallas_call(
        kernel,
        out_shape=jax.ShapeDtypeStruct(pos.shape, pos.dtype),
        in_specs=[SMEM],
        out_specs=SMEM,
        cost_estimate=pl.CostEstimate(flops=40_000_000_000, bytes_accessed=100_000_000, transcendentals=0),
        name="meanwhile",
    )(pos)


def rows_kernel(pos_ref, mine_ref, other_ref, l_ref, w_ref, p_hbm, q_hbm, p_ref, q_ref, p_sem, q_sem):
    r = pos_ref[0]
    c = pos_ref[1]
    n = 2 * NB
    lane0 = c % 2 == 0
    copies = []
    panels = []
    for k in range(4):
        at = slice(k * NB, (k + 1) * NB)
        mine = mine_ref[at, :]
        other = other_ref[at, :]
        g0 = jnp.where(lane0, mine, other)
        g1 = jnp.where(lane0, other, mine)
        p0 = dot_nt(g0, w_ref[:NB, :NB])
        p1 = dot_nt(jnp.concatenate([g0, g1], axis=1), w_ref[NB:, :])
        q0 = dot_nn(jnp.concatenate([p0, p1], axis=1), w_ref[:, :NB])
        q1 = dot_nn(p1, w_ref[NB:, NB:])
        for h, part in enumerate(split3(jnp.concatenate([q0, q1], axis=1))):
            q_ref[at, h * n:(h + 1) * n] = part.astype(BF16)
        copies.append(pltpu.make_async_copy(q_ref.at[at], q_hbm.at[at], q_sem.at[k]))
        copies[-1].start()
        p = jnp.where(c == 0, p0, p1)
        if k == 0:
            zero = jnp.zeros((NB, NB), F32)
            p = jnp.where(r == 0, jnp.where(c == 0, l_ref[:NB, :NB], zero), p)
            p = jnp.where(r == 1, jnp.where(c == 0, l_ref[NB:, :NB], l_ref[NB:, NB:]), p)
        p_ref[at, :] = p
        panels.append(pltpu.make_async_copy(p_ref.at[at], p_hbm.at[at], p_sem.at[k]))
        pl.when(c < 2)(panels[-1].start)
    for copy in copies:
        copy.wait()

    @pl.when(c < 2)
    def _():
        for copy in panels:
            copy.wait()


def solve_rows(pos, mine, other, factors):
    hbm = pl.BlockSpec(memory_space=pltpu.HBM)
    p = jax.ShapeDtypeStruct((4 * NB, NB), F32)
    q = jax.ShapeDtypeStruct((4 * NB, 6 * NB), BF16)
    return pl.pallas_call(
        rows_kernel,
        out_shape=[pltpu.HBM(p.shape, F32), pltpu.HBM(q.shape, BF16)],
        in_specs=[SMEM] + [VMEM] * 4,
        out_specs=[hbm] * 2,
        scratch_shapes=[
            pltpu.VMEM(p.shape, F32),
            pltpu.VMEM(q.shape, BF16),
            pltpu.SemaphoreType.DMA((4,)),
            pltpu.SemaphoreType.DMA((4,)),
        ],
        compiler_params=pltpu.CompilerParams(vmem_limit_bytes=20 * 2**20),
        cost_estimate=pl.CostEstimate(flops=1_000_000, bytes_accessed=5_000_000, transcendentals=0),
        name="solve_rows",
    )(pos, mine, other, *factors)


def update_kernel(pos_ref, a_hbm, p_hbm, q_hbm, gc_ref, o_hbm, a_ref, q_ref, g_ref, o_ref, load_sems, store_sems, panel_sem):
    r = pos_ref[0]
    c = pos_ref[1]
    n = 2 * NB
    order = (3, 2, 1, 0)
    part = [slice(k * NB, (k + 1) * NB) for k in range(4)]
    loads = {
        k: [
            pltpu.make_async_copy(q_hbm.at[part[k]], q_ref.at[part[k]], load_sems.at[0, k]),
            pltpu.make_async_copy(a_hbm.at[part[k]], a_ref.at[part[k]], load_sems.at[1, k]),
        ]
        for k in order
    }
    for copy in loads[3]:
        copy.start()
    panel = pltpu.make_async_copy(p_hbm, o_ref.at[:, :NB], panel_sem)

    @pl.when(c < 2)
    def _():
        panel.start()

    for k in order[1:]:
        for copy in loads[k]:
            copy.start()

    def block(k, m):
        small = dot_nt_16(q_ref[part[k], :], g_ref[part[m], :])
        small += dot_nt_16(q_ref[part[k], :2 * n], g_ref[part[m], n:])
        main = dot_nt_16(q_ref[part[k], :n], g_ref[part[m], 2 * n:])
        o_ref[part[k], part[m]] = a_ref[part[k], part[m]] - (small + main)

    def clear(k, m):
        o_ref[part[k], part[m]] = jnp.zeros((NB, NB), F32)

    def split(m):
        core = c % 2
        for h, lane in enumerate((core, 1 - core)):
            hi, mid, lo = split3(gc_ref[:, lane, m].reshape(NB, NB))
            for k, piece in enumerate((lo, mid, hi)):
                g_ref[part[m], k * n + h * NB:k * n + (h + 1) * NB] = piece.astype(BF16)

    pl.when(c >= 2)(lambda: split(0))
    for m in range(1, 4):
        split(m)
        for k in range(m):
            clear(k, m)

    stores = []
    for k in order:
        for copy in loads[k]:
            copy.wait()
        for m in range(1, k):
            block(k, m)

        @pl.when(c >= 2)
        def _():
            if k > 0:
                block(k, 0)

        if k == 3:
            @pl.when(c < 2)
            def _():
                panel.wait()

        inside = r >= c if k > 0 else (r >= c) & (c >= 2)
        outside = r < c if k > 0 else (r < c) & (c >= 2)

        @pl.when(inside)
        def _():
            block(k, k)

        @pl.when(outside)
        def _():
            clear(k, k)

        stores.append(pltpu.make_async_copy(o_ref.at[part[k]], o_hbm.at[part[k]], store_sems.at[k]))
        stores[-1].start()
    for copy in stores:
        copy.wait()


def update(pos, a, p, q, gc):
    hbm = pl.BlockSpec(memory_space=pltpu.HBM)
    return pl.pallas_call(
        update_kernel,
        out_shape=jax.ShapeDtypeStruct(a.shape, F32),
        in_specs=[SMEM, hbm, hbm, hbm, VMEM],
        out_specs=hbm,
        scratch_shapes=[
            pltpu.VMEM(a.shape, F32),
            pltpu.VMEM(q.shape, BF16),
            pltpu.VMEM(q.shape, BF16),
            pltpu.VMEM(a.shape, F32),
            pltpu.SemaphoreType.DMA((2, 4)),
            pltpu.SemaphoreType.DMA((4,)),
            pltpu.SemaphoreType.DMA(()),
        ],
        compiler_params=pltpu.CompilerParams(vmem_limit_bytes=32 * 2**20),
        cost_estimate=pl.CostEstimate(flops=8_000_000_000, bytes_accessed=13_000_000, transcendentals=0),
        name="update",
    )(pos, a, p, q, gc)


TREE = (
    tuple(((0, d or 4),) for d in range(8)),
    (
        ((0, 6), (4, 2)), ((0, 6), (1, 3)), ((0, 6), (2, 4)), ((0, 6), (3, 5)),
        ((0, 2), (4, 6)), ((0, 2), (5, 3)), ((0, 2), (6, 4)), ((0, 2), (7, 5)),
    ),
    (
        ((0, 7), (6, 5), (4, 3), (2, 1)), ((0, 7), (1, 2), (3, 4), (6, 5)),
        ((0, 1), (2, 3), (4, 5), (6, 7)), ((0, 1), (3, 2), (5, 4), (6, 7)),
        ((0, 1), (2, 3), (4, 5), (6, 7)), ((0, 7), (2, 1), (3, 4), (5, 6)),
        ((0, 1), (2, 3), (4, 5), (6, 7)), ((0, 1), (2, 3), (5, 4), (7, 6)),
    ),
)


LEAD = (((0, 5),), ((0, 7), (5, 3)), ((0, 1), (7, 6), (5, 4), (3, 2)))


def along_z(x, moves):
    pairs = [(16 * r + 2 * a + h, 16 * r + 2 * b + h) for r in range(16) for a, b in moves(r // 2) for h in range(2)]
    return lax.ppermute(x, ("row", "col"), pairs)


def per_device(a):
    r = lax.axis_index("row").astype(jnp.int32)
    c = lax.axis_index("col").astype(jnp.int32)
    pos = jnp.stack([r, c])
    swap = [(i, i ^ 1) for i in range(16)]
    x = a[:, :NB]
    here = c < 2

    lead = lax.all_to_all(x[:NB].reshape(16, 16, NB), "row", 0, 0, tiled=True)[0:2].reshape(32, NB)
    lead = jnp.where(here, lead, 0.0)
    for moves in LEAD:
        lead += along_z(lead, lambda d: moves if d < 5 else [((8 - s) % 8, (8 - t) % 8) for s, t in moves])
    panel = jnp.where(here, x, 0.0)
    panel += along_z(panel, lambda d: TREE[0][d])
    lead, panel, pos = lax.optimization_barrier((lead, panel, pos))

    pieces = panel.reshape(4, 16, 16, NB).transpose(1, 0, 2, 3).reshape(16, 64, NB)
    pieces = jnp.concatenate([pieces, jnp.broadcast_to(lead[None], (16, 32, NB))], axis=1)
    held = lax.all_to_all(pieces, "row", 0, 0, tiled=True)
    arrived, pos = lax.optimization_barrier((along_z(panel, lambda d: TREE[1][d]), meanwhile(pos)))
    panel += arrived
    arrived = along_z(panel, lambda d: TREE[2][d])
    held, panel, pos = lax.optimization_barrier((held, panel, pos))

    lead = held[:, 64:].reshape(16, 2, 16, NB)
    theirs = lax.ppermute(lead, "col", swap)
    mine = lax.dynamic_index_in_dim(held, c, 0, keepdims=False)[:64]
    other = lax.ppermute(lax.dynamic_index_in_dim(held, c ^ 1, 0, keepdims=False)[:64], "col", swap)
    mine, other, lead, theirs, panel = lax.optimization_barrier((mine, other, lead, theirs, panel))
    gc = jnp.stack([mine, other]).reshape(2, 4, 16, NB)
    gc = lax.all_to_all(jnp.broadcast_to(gc[None], (16, 2, 4, 16, NB)), "row", 0, 0, tiled=True)
    *factors, arrived = lax.optimization_barrier((*factor(pos, lead, theirs), arrived))
    panel += arrived
    p, q = solve_rows(pos, panel, lax.ppermute(panel, "col", swap), factors)
    a, p, q = (pltpu.with_memory_space_constraint(v, pltpu.HBM) for v in (a, p, q))
    return update(pos, a, p, q, gc)


def solution(mesh):
    return jax.shard_map(
        per_device,
        mesh=mesh,
        in_specs=(P("row", "col"),),
        out_specs=P("row", "col"),
        check_vma=False,
    )
```

```python
import jax
import jax.numpy as jnp
from jax import lax
from jax.experimental import pallas as pl
from jax.experimental.pallas import tpu as pltpu
from jax.sharding import PartitionSpec as P

NB = 256
HB = 128
STEP = 16
HIGH = lax.Precision.HIGHEST
F32 = jnp.float32
BF16 = jnp.bfloat16
VMEM = pl.BlockSpec(memory_space=pltpu.VMEM)
SMEM = pl.BlockSpec(memory_space=pltpu.SMEM)


def dot_nt(a, b):
    return lax.dot_general(a, b, (((1,), (1,)), ((), ())), precision=HIGH, preferred_element_type=F32)


def dot_nn(a, b):
    return lax.dot_general(a, b, (((1,), (0,)), ((), ())), precision=HIGH, preferred_element_type=F32)


def dot_tn(a, b):
    return lax.dot_general(a, b, (((0,), (0,)), ((), ())), precision=HIGH, preferred_element_type=F32)


def dot_nt_16(a, b):
    return lax.dot_general(a, b, (((1,), (1,)), ((), ())), preferred_element_type=F32)


def split3(x):
    hi = x.astype(BF16).astype(F32)
    rest = x - hi
    mid = rest.astype(BF16).astype(F32)
    return hi, mid, rest - mid


def dot_tn_short(a, b):
    ah, am, al = split3(a)
    bh, bm, bl = split3(b)
    left = jnp.concatenate([ah, ah, am, ah, al, am], axis=0).astype(BF16)
    right = jnp.concatenate([bh, bm, bh, bl, bh, bm], axis=0).astype(BF16)
    return lax.dot_general(left, right, (((0,), (0,)), ((), ())), preferred_element_type=F32)


def reciprocal(x):
    r = pl.reciprocal(x, approx=True)
    return r * (2.0 - x * r)


def inverse_root(x):
    r = lax.rsqrt(x)
    return r * (1.5 - 0.5 * x * r * r)


def factor_half(m_ref):
    sub = lax.broadcasted_iota(jnp.int32, (STEP, HB), 0)
    lane = lax.broadcasted_iota(jnp.int32, (STEP, HB), 1)
    odd = (sub & 1) == 1

    def spread(x, i):
        return jnp.broadcast_to(x[i:i + 1, :], (STEP, HB))

    for lo in range(0, HB, STEP):
        s = m_ref[lo:lo + STEP, :HB]
        v = m_ref[lo:lo + STEP, HB:]
        cols = [jnp.broadcast_to(s[:, lo + j:lo + j + 1], (STEP, HB)) for j in range(STEP)]
        first = jnp.ones((STEP, HB), F32)
        dets = first
        cross = first
        for j in range(0, STEP, 2):
            a, b, c = spread(cols[j], j), spread(cols[j], j + 1), spread(cols[j + 1], j + 1)
            det = a * c - b * b
            pair = (sub == j) | (sub == j + 1)
            first = jnp.where(pair, a, first)
            dets = jnp.where(pair, det, dets)
            cross = jnp.where(pair, b, cross)
            if j < STEP - 2:
                r = reciprocal(det)
                below = sub > j + 1
                f0 = jnp.where(below, (cols[j] * c - cols[j + 1] * b) * r, 0.0)
                f1 = jnp.where(below, (cols[j + 1] * a - cols[j] * b) * r, 0.0)
                for i in range(j + 2, STEP):
                    cols[i] = cols[i] - (f0 * spread(cols[i], j) + f1 * spread(cols[i], j + 1))
                s = s - (f0 * spread(s, j) + f1 * spread(s, j + 1))
                v = v - (f0 * spread(v, j) + f1 * spread(v, j + 1))
        ra = inverse_root(first)
        scale = jnp.where(odd, first * ra * inverse_root(dets), ra)
        mult = jnp.where(odd, cross * ra * ra, 0.0)
        s = jnp.where(lane >= lo + sub, (s - mult * pltpu.roll(s, 1, 0)) * scale, 0.0)
        v = (v - mult * pltpu.roll(v, 1, 0)) * scale
        uw = jnp.concatenate([s, v], axis=1)
        m_ref[lo:lo + STEP, :] = uw
        if lo + STEP < HB:
            full = dot_tn_short(s, uw)
            m_ref[lo + STEP:, :] = m_ref[lo + STEP:, :] - full[lo + STEP:, :]


def factor_kernel(pos_ref, mine_ref, theirs_ref, l_ref, w_ref, a_ref, s_ref, m_ref):
    lane0 = pos_ref[1] % 2 == 0
    for k in range(16):
        at = slice(16 * k, 16 * k + 16)
        mine = mine_ref[k]
        theirs = theirs_ref[k]
        a_ref[0, at, :] = jnp.where(lane0, mine[0], theirs[0])
        a_ref[1, at, :] = jnp.where(lane0, mine[1], theirs[1])
        a_ref[2, at, :] = jnp.where(lane0, theirs[1], mine[1])
    a00 = a_ref[0]
    a11 = a_ref[2]
    s_ref[:NB, :NB] = (a00 + a00.T) * 0.5
    s_ref[:NB, NB:] = a_ref[1].T
    s_ref[NB:, NB:] = (a11 + a11.T) * 0.5
    eye = (lax.broadcasted_iota(jnp.int32, (HB, HB), 0) == lax.broadcasted_iota(jnp.int32, (HB, HB), 1)).astype(F32)
    l_ref[...] = jnp.zeros((2 * NB, 2 * NB), F32)
    w_ref[...] = jnp.zeros((2 * NB, 2 * NB), F32)
    for k in range(4):
        lo = k * HB
        hi = lo + HB
        m_ref[:, :HB] = s_ref[lo:hi, lo:hi]
        m_ref[:, HB:] = eye
        factor_half(m_ref)
        w = m_ref[:, HB:]
        l_ref[lo:hi, lo:hi] = m_ref[:, :HB].T
        w_ref[lo:hi, lo:hi] = w
        if k < 3:
            row = dot_nn(w, s_ref[lo:hi, hi:])
            s_ref[lo:hi, hi:] = row
            s_ref[hi:, hi:] = s_ref[hi:, hi:] - dot_tn(row, row)
            l_ref[hi:, lo:hi] = row.T
        if k % 2 == 1:
            w_ref[lo:hi, lo - HB:lo] = -dot_nn(w, dot_nn(l_ref[lo:hi, lo - HB:lo], w_ref[lo - HB:lo, lo - HB:lo]))
    w_ref[NB:, :NB] = -dot_nn(w_ref[NB:, NB:], dot_nn(l_ref[NB:, :NB], w_ref[:NB, :NB]))


def factor(pos, mine, theirs):
    both = jax.ShapeDtypeStruct((2 * NB, 2 * NB), F32)
    return pl.pallas_call(
        factor_kernel,
        out_shape=[both] * 2,
        in_specs=[SMEM, VMEM, VMEM],
        out_specs=[VMEM] * 2,
        scratch_shapes=[
            pltpu.VMEM((3, NB, NB), F32),
            pltpu.VMEM((2 * NB, 2 * NB), F32),
            pltpu.VMEM((HB, 2 * HB), F32),
        ],
        compiler_params=pltpu.CompilerParams(vmem_limit_bytes=16 * 2**20),
        cost_estimate=pl.CostEstimate(flops=1_000_000, bytes_accessed=4_000_000, transcendentals=0),
        name="factor_lead",
    )(pos, mine, theirs)


def meanwhile(pos):
    def kernel(x_ref, o_ref):
        o_ref[0] = x_ref[0]
        o_ref[1] = x_ref[1]

    return pl.pallas_call(
        kernel,
        out_shape=jax.ShapeDtypeStruct(pos.shape, pos.dtype),
        in_specs=[SMEM],
        out_specs=SMEM,
        cost_estimate=pl.CostEstimate(flops=40_000_000_000, bytes_accessed=100_000_000, transcendentals=0),
        name="meanwhile",
    )(pos)


def rows_kernel(pos_ref, mine_ref, other_ref, l_ref, w_ref, p_hbm, q_hbm, p_ref, q_ref, p_sem, q_sem):
    r = pos_ref[0]
    c = pos_ref[1]
    n = 2 * NB
    lane0 = c % 2 == 0
    copies = []
    panels = []
    for k in range(4):
        at = slice(k * NB, (k + 1) * NB)
        mine = mine_ref[at, :]
        other = other_ref[at, :]
        g0 = jnp.where(lane0, mine, other)
        g1 = jnp.where(lane0, other, mine)
        p0 = dot_nt(g0, w_ref[:NB, :NB])
        p1 = dot_nt(jnp.concatenate([g0, g1], axis=1), w_ref[NB:, :])
        q0 = dot_nn(jnp.concatenate([p0, p1], axis=1), w_ref[:, :NB])
        q1 = dot_nn(p1, w_ref[NB:, NB:])
        for h, part in enumerate(split3(jnp.concatenate([q0, q1], axis=1))):
            q_ref[at, h * n:(h + 1) * n] = part.astype(BF16)
        copies.append(pltpu.make_async_copy(q_ref.at[at], q_hbm.at[at], q_sem.at[k]))
        copies[-1].start()
        p = jnp.where(c == 0, p0, p1)
        if k == 0:
            zero = jnp.zeros((NB, NB), F32)
            p = jnp.where(r == 0, jnp.where(c == 0, l_ref[:NB, :NB], zero), p)
            p = jnp.where(r == 1, jnp.where(c == 0, l_ref[NB:, :NB], l_ref[NB:, NB:]), p)
        p_ref[at, :] = p
        panels.append(pltpu.make_async_copy(p_ref.at[at], p_hbm.at[at], p_sem.at[k]))
        pl.when(c < 2)(panels[-1].start)
    for copy in copies:
        copy.wait()

    @pl.when(c < 2)
    def _():
        for copy in panels:
            copy.wait()


def solve_rows(pos, mine, other, factors):
    hbm = pl.BlockSpec(memory_space=pltpu.HBM)
    p = jax.ShapeDtypeStruct((4 * NB, NB), F32)
    q = jax.ShapeDtypeStruct((4 * NB, 6 * NB), BF16)
    return pl.pallas_call(
        rows_kernel,
        out_shape=[pltpu.HBM(p.shape, F32), pltpu.HBM(q.shape, BF16)],
        in_specs=[SMEM] + [VMEM] * 4,
        out_specs=[hbm] * 2,
        scratch_shapes=[
            pltpu.VMEM(p.shape, F32),
            pltpu.VMEM(q.shape, BF16),
            pltpu.SemaphoreType.DMA((4,)),
            pltpu.SemaphoreType.DMA((4,)),
        ],
        compiler_params=pltpu.CompilerParams(vmem_limit_bytes=20 * 2**20),
        cost_estimate=pl.CostEstimate(flops=1_000_000, bytes_accessed=5_000_000, transcendentals=0),
        name="solve_rows",
    )(pos, mine, other, *factors)


def update_kernel(pos_ref, a_hbm, p_hbm, q_hbm, gc_ref, o_hbm, a_ref, q_ref, g_ref, o_ref, load_sems, store_sems, panel_sem):
    r = pos_ref[0]
    c = pos_ref[1]
    n = 2 * NB
    order = (3, 2, 1, 0)
    part = [slice(k * NB, (k + 1) * NB) for k in range(4)]
    loads = {
        k: [
            pltpu.make_async_copy(q_hbm.at[part[k]], q_ref.at[part[k]], load_sems.at[0, k]),
            pltpu.make_async_copy(a_hbm.at[part[k]], a_ref.at[part[k]], load_sems.at[1, k]),
        ]
        for k in order
    }
    for copy in loads[3]:
        copy.start()
    panel = pltpu.make_async_copy(p_hbm, o_ref.at[:, :NB], panel_sem)

    @pl.when(c < 2)
    def _():
        panel.start()

    for k in order[1:]:
        for copy in loads[k]:
            copy.start()

    def block(k, m):
        small = dot_nt_16(q_ref[part[k], :], g_ref[part[m], :])
        small += dot_nt_16(q_ref[part[k], :2 * n], g_ref[part[m], n:])
        main = dot_nt_16(q_ref[part[k], :n], g_ref[part[m], 2 * n:])
        o_ref[part[k], part[m]] = a_ref[part[k], part[m]] - (small + main)

    def clear(k, m):
        o_ref[part[k], part[m]] = jnp.zeros((NB, NB), F32)

    def split(m):
        core = c % 2
        for h, lane in enumerate((core, 1 - core)):
            hi, mid, lo = split3(gc_ref[:, lane, m].reshape(NB, NB))
            for k, piece in enumerate((lo, mid, hi)):
                g_ref[part[m], k * n + h * NB:k * n + (h + 1) * NB] = piece.astype(BF16)

    split(1)
    for m in range(1, 4):
        for k in range(m):
            clear(k, m)

    stores = []
    for k in order:
        for copy in loads[k]:
            copy.wait()
        for m in range(1, k):
            block(k, m)
            if k == 3:
                split(m + 1)

        @pl.when(c >= 2)
        def _():
            if k == 3:
                split(0)
            if k > 0:
                block(k, 0)

        if k == 3:
            @pl.when(c < 2)
            def _():
                panel.wait()

        inside = r >= c if k > 0 else (r >= c) & (c >= 2)
        outside = r < c if k > 0 else (r < c) & (c >= 2)

        @pl.when(inside)
        def _():
            block(k, k)

        @pl.when(outside)
        def _():
            clear(k, k)

        stores.append(pltpu.make_async_copy(o_ref.at[part[k]], o_hbm.at[part[k]], store_sems.at[k]))
        stores[-1].start()
    for copy in stores:
        copy.wait()


def update(pos, a, p, q, gc):
    hbm = pl.BlockSpec(memory_space=pltpu.HBM)
    return pl.pallas_call(
        update_kernel,
        out_shape=jax.ShapeDtypeStruct(a.shape, F32),
        in_specs=[SMEM, hbm, hbm, hbm, VMEM],
        out_specs=hbm,
        scratch_shapes=[
            pltpu.VMEM(a.shape, F32),
            pltpu.VMEM(q.shape, BF16),
            pltpu.VMEM(q.shape, BF16),
            pltpu.VMEM(a.shape, F32),
            pltpu.SemaphoreType.DMA((2, 4)),
            pltpu.SemaphoreType.DMA((4,)),
            pltpu.SemaphoreType.DMA(()),
        ],
        compiler_params=pltpu.CompilerParams(vmem_limit_bytes=32 * 2**20),
        cost_estimate=pl.CostEstimate(flops=8_000_000_000, bytes_accessed=13_000_000, transcendentals=0),
        name="update",
    )(pos, a, p, q, gc)


TREE = (
    tuple(((0, d or 4),) for d in range(8)),
    (
        ((0, 6), (4, 2)), ((0, 6), (1, 3)), ((0, 6), (2, 4)), ((0, 6), (3, 5)),
        ((0, 2), (4, 6)), ((0, 2), (5, 3)), ((0, 2), (6, 4)), ((0, 2), (7, 5)),
    ),
    (
        ((0, 7), (6, 5), (4, 3), (2, 1)), ((0, 7), (1, 2), (3, 4), (6, 5)),
        ((0, 1), (2, 3), (4, 5), (6, 7)), ((0, 1), (3, 2), (5, 4), (6, 7)),
        ((0, 1), (2, 3), (4, 5), (6, 7)), ((0, 7), (2, 1), (3, 4), (5, 6)),
        ((0, 1), (2, 3), (4, 5), (6, 7)), ((0, 1), (2, 3), (5, 4), (7, 6)),
    ),
)


LEAD = (((0, 5),), ((0, 7), (5, 3)), ((0, 1), (7, 6), (5, 4), (3, 2)))


def along_z(x, moves):
    pairs = [(16 * r + 2 * a + h, 16 * r + 2 * b + h) for r in range(16) for a, b in moves(r // 2) for h in range(2)]
    return lax.ppermute(x, ("row", "col"), pairs)


def per_device(a):
    r = lax.axis_index("row").astype(jnp.int32)
    c = lax.axis_index("col").astype(jnp.int32)
    pos = jnp.stack([r, c])
    swap = [(i, i ^ 1) for i in range(16)]
    x = a[:, :NB]
    here = c < 2

    lead = lax.all_to_all(x[:NB].reshape(16, 16, NB), "row", 0, 0, tiled=True)[0:2].reshape(32, NB)
    lead = jnp.where(here, lead, 0.0)
    for moves in LEAD:
        lead += along_z(lead, lambda d: moves if d < 5 else [((8 - s) % 8, (8 - t) % 8) for s, t in moves])
    panel = jnp.where(here, x, 0.0)
    panel += along_z(panel, lambda d: TREE[0][d])
    lead, panel, pos = lax.optimization_barrier((lead, panel, pos))

    pieces = panel.reshape(4, 16, 16, NB).transpose(1, 0, 2, 3).reshape(16, 64, NB)
    pieces = jnp.concatenate([pieces, jnp.broadcast_to(lead[None], (16, 32, NB))], axis=1)
    held = lax.all_to_all(pieces, "row", 0, 0, tiled=True)
    arrived, pos = lax.optimization_barrier((along_z(panel, lambda d: TREE[1][d]), meanwhile(pos)))
    panel += arrived
    arrived = along_z(panel, lambda d: TREE[2][d])
    held, panel, pos = lax.optimization_barrier((held, panel, pos))

    lead = held[:, 64:].reshape(16, 2, 16, NB)
    theirs = lax.ppermute(lead, "col", swap)
    mine = lax.dynamic_index_in_dim(held, c, 0, keepdims=False)[:64]
    other = lax.ppermute(lax.dynamic_index_in_dim(held, c ^ 1, 0, keepdims=False)[:64], "col", swap)
    mine, other, lead, theirs, panel = lax.optimization_barrier((mine, other, lead, theirs, panel))
    gc = jnp.stack([mine, other]).reshape(2, 4, 16, NB)
    gc = lax.all_to_all(jnp.broadcast_to(gc[None], (16, 2, 4, 16, NB)), "row", 0, 0, tiled=True)
    *factors, arrived = lax.optimization_barrier((*factor(pos, lead, theirs), arrived))
    panel += arrived
    p, q = solve_rows(pos, panel, lax.ppermute(panel, "col", swap), factors)
    a, p, q = (pltpu.with_memory_space_constraint(v, pltpu.HBM) for v in (a, p, q))
    return update(pos, a, p, q, gc)


def solution(mesh):
    return jax.shard_map(
        per_device,
        mesh=mesh,
        in_specs=(P("row", "col"),),
        out_specs=P("row", "col"),
        check_vma=False,
    )
```

```python
import jax
import jax.numpy as jnp
from jax import lax
from jax.experimental import pallas as pl
from jax.experimental.pallas import tpu as pltpu
from jax.sharding import PartitionSpec as P

NB = 256
HB = 128
STEP = 16
HIGH = lax.Precision.HIGHEST
F32 = jnp.float32
BF16 = jnp.bfloat16
VMEM = pl.BlockSpec(memory_space=pltpu.VMEM)
SMEM = pl.BlockSpec(memory_space=pltpu.SMEM)


def dot_nt(a, b):
    return lax.dot_general(a, b, (((1,), (1,)), ((), ())), precision=HIGH, preferred_element_type=F32)


def dot_nn(a, b):
    return lax.dot_general(a, b, (((1,), (0,)), ((), ())), precision=HIGH, preferred_element_type=F32)


def dot_tn(a, b):
    return lax.dot_general(a, b, (((0,), (0,)), ((), ())), precision=HIGH, preferred_element_type=F32)


def dot_nt_16(a, b):
    return lax.dot_general(a, b, (((1,), (1,)), ((), ())), preferred_element_type=F32)


def split3(x):
    hi = x.astype(BF16).astype(F32)
    rest = x - hi
    mid = rest.astype(BF16).astype(F32)
    return hi, mid, rest - mid


def dot_tn_short(a, b):
    ah, am, al = split3(a)
    bh, bm, bl = split3(b)
    left = jnp.concatenate([ah, ah, am, ah, al, am], axis=0).astype(BF16)
    right = jnp.concatenate([bh, bm, bh, bl, bh, bm], axis=0).astype(BF16)
    return lax.dot_general(left, right, (((0,), (0,)), ((), ())), preferred_element_type=F32)


def reciprocal(x):
    r = pl.reciprocal(x, approx=True)
    return r * (2.0 - x * r)


def inverse_root(x):
    r = lax.rsqrt(x)
    return r * (1.5 - 0.5 * x * r * r)


def factor_half(m_ref):
    sub = lax.broadcasted_iota(jnp.int32, (STEP, HB), 0)
    lane = lax.broadcasted_iota(jnp.int32, (STEP, HB), 1)
    odd = (sub & 1) == 1

    def spread(x, i):
        return jnp.broadcast_to(x[i:i + 1, :], (STEP, HB))

    for lo in range(0, HB, STEP):
        s = m_ref[lo:lo + STEP, :HB]
        v = m_ref[lo:lo + STEP, HB:]
        cols = [jnp.broadcast_to(s[:, lo + j:lo + j + 1], (STEP, HB)) for j in range(STEP)]
        first = jnp.ones((STEP, HB), F32)
        dets = first
        cross = first
        for j in range(0, STEP, 2):
            a, b, c = spread(cols[j], j), spread(cols[j], j + 1), spread(cols[j + 1], j + 1)
            det = a * c - b * b
            pair = (sub == j) | (sub == j + 1)
            first = jnp.where(pair, a, first)
            dets = jnp.where(pair, det, dets)
            cross = jnp.where(pair, b, cross)
            if j < STEP - 2:
                r = reciprocal(det)
                below = sub > j + 1
                f0 = jnp.where(below, (cols[j] * c - cols[j + 1] * b) * r, 0.0)
                f1 = jnp.where(below, (cols[j + 1] * a - cols[j] * b) * r, 0.0)
                for i in range(j + 2, STEP):
                    cols[i] = cols[i] - (f0 * spread(cols[i], j) + f1 * spread(cols[i], j + 1))
                s = s - (f0 * spread(s, j) + f1 * spread(s, j + 1))
                v = v - (f0 * spread(v, j) + f1 * spread(v, j + 1))
        ra = inverse_root(first)
        scale = jnp.where(odd, first * ra * inverse_root(dets), ra)
        mult = jnp.where(odd, cross * ra * ra, 0.0)
        s = jnp.where(lane >= lo + sub, (s - mult * pltpu.roll(s, 1, 0)) * scale, 0.0)
        v = (v - mult * pltpu.roll(v, 1, 0)) * scale
        uw = jnp.concatenate([s, v], axis=1)
        m_ref[lo:lo + STEP, :] = uw
        if lo + STEP < HB:
            full = dot_tn_short(s, uw)
            m_ref[lo + STEP:, :] = m_ref[lo + STEP:, :] - full[lo + STEP:, :]


def factor_kernel(pos_ref, mine_ref, theirs_ref, l_ref, w_ref, a_ref, s_ref, m_ref):
    lane0 = pos_ref[1] % 2 == 0
    for k in range(16):
        at = slice(16 * k, 16 * k + 16)
        mine = mine_ref[k]
        theirs = theirs_ref[k]
        a_ref[0, at, :] = jnp.where(lane0, mine[0], theirs[0])
        a_ref[1, at, :] = jnp.where(lane0, mine[1], theirs[1])
        a_ref[2, at, :] = jnp.where(lane0, theirs[1], mine[1])
    a00 = a_ref[0]
    a11 = a_ref[2]
    s_ref[:NB, :NB] = (a00 + a00.T) * 0.5
    s_ref[:NB, NB:] = a_ref[1].T
    s_ref[NB:, NB:] = (a11 + a11.T) * 0.5
    eye = (lax.broadcasted_iota(jnp.int32, (HB, HB), 0) == lax.broadcasted_iota(jnp.int32, (HB, HB), 1)).astype(F32)
    l_ref[...] = jnp.zeros((2 * NB, 2 * NB), F32)
    w_ref[...] = jnp.zeros((2 * NB, 2 * NB), F32)
    for k in range(4):
        lo = k * HB
        hi = lo + HB
        m_ref[:, :HB] = s_ref[lo:hi, lo:hi]
        m_ref[:, HB:] = eye
        factor_half(m_ref)
        w = m_ref[:, HB:]
        l_ref[lo:hi, lo:hi] = m_ref[:, :HB].T
        w_ref[lo:hi, lo:hi] = w
        if k < 3:
            row = dot_nn(w, s_ref[lo:hi, hi:])
            s_ref[lo:hi, hi:] = row
            for at in range(hi, 2 * NB, HB):
                s_ref[at:at + HB, at:] = s_ref[at:at + HB, at:] - dot_tn(row[:, at - hi:at - hi + HB], row[:, at - hi:])
            l_ref[hi:, lo:hi] = row.T
        if k % 2 == 1:
            w_ref[lo:hi, lo - HB:lo] = -dot_nn(w, dot_nn(l_ref[lo:hi, lo - HB:lo], w_ref[lo - HB:lo, lo - HB:lo]))
    w_ref[NB:, :NB] = -dot_nn(w_ref[NB:, NB:], dot_nn(l_ref[NB:, :NB], w_ref[:NB, :NB]))


def factor(pos, mine, theirs):
    both = jax.ShapeDtypeStruct((2 * NB, 2 * NB), F32)
    return pl.pallas_call(
        factor_kernel,
        out_shape=[both] * 2,
        in_specs=[SMEM, VMEM, VMEM],
        out_specs=[VMEM] * 2,
        scratch_shapes=[
            pltpu.VMEM((3, NB, NB), F32),
            pltpu.VMEM((2 * NB, 2 * NB), F32),
            pltpu.VMEM((HB, 2 * HB), F32),
        ],
        compiler_params=pltpu.CompilerParams(vmem_limit_bytes=16 * 2**20),
        cost_estimate=pl.CostEstimate(flops=1_000_000, bytes_accessed=4_000_000, transcendentals=0),
        name="factor_lead",
    )(pos, mine, theirs)


def meanwhile(pos):
    def kernel(x_ref, o_ref):
        o_ref[0] = x_ref[0]
        o_ref[1] = x_ref[1]

    return pl.pallas_call(
        kernel,
        out_shape=jax.ShapeDtypeStruct(pos.shape, pos.dtype),
        in_specs=[SMEM],
        out_specs=SMEM,
        cost_estimate=pl.CostEstimate(flops=40_000_000_000, bytes_accessed=100_000_000, transcendentals=0),
        name="meanwhile",
    )(pos)


def rows_kernel(pos_ref, mine_ref, other_ref, l_ref, w_ref, p_hbm, q_hbm, p_ref, q_ref, p_sem, q_sem):
    r = pos_ref[0]
    c = pos_ref[1]
    n = 2 * NB
    lane0 = c % 2 == 0
    copies = []
    panels = []
    for k in range(4):
        at = slice(k * NB, (k + 1) * NB)
        mine = mine_ref[at, :]
        other = other_ref[at, :]
        g0 = jnp.where(lane0, mine, other)
        g1 = jnp.where(lane0, other, mine)
        p0 = dot_nt(g0, w_ref[:NB, :NB])
        p1 = dot_nt(jnp.concatenate([g0, g1], axis=1), w_ref[NB:, :])
        q0 = dot_nn(jnp.concatenate([p0, p1], axis=1), w_ref[:, :NB])
        q1 = dot_nn(p1, w_ref[NB:, NB:])
        for h, part in enumerate(split3(jnp.concatenate([q0, q1], axis=1))):
            q_ref[at, h * n:(h + 1) * n] = part.astype(BF16)
        copies.append(pltpu.make_async_copy(q_ref.at[at], q_hbm.at[at], q_sem.at[k]))
        copies[-1].start()
        p = jnp.where(c == 0, p0, p1)
        if k == 0:
            zero = jnp.zeros((NB, NB), F32)
            p = jnp.where(r == 0, jnp.where(c == 0, l_ref[:NB, :NB], zero), p)
            p = jnp.where(r == 1, jnp.where(c == 0, l_ref[NB:, :NB], l_ref[NB:, NB:]), p)
        p_ref[at, :] = p
        panels.append(pltpu.make_async_copy(p_ref.at[at], p_hbm.at[at], p_sem.at[k]))
        pl.when(c < 2)(panels[-1].start)
    for copy in copies:
        copy.wait()

    @pl.when(c < 2)
    def _():
        for copy in panels:
            copy.wait()


def solve_rows(pos, mine, other, factors):
    hbm = pl.BlockSpec(memory_space=pltpu.HBM)
    p = jax.ShapeDtypeStruct((4 * NB, NB), F32)
    q = jax.ShapeDtypeStruct((4 * NB, 6 * NB), BF16)
    return pl.pallas_call(
        rows_kernel,
        out_shape=[pltpu.HBM(p.shape, F32), pltpu.HBM(q.shape, BF16)],
        in_specs=[SMEM] + [VMEM] * 4,
        out_specs=[hbm] * 2,
        scratch_shapes=[
            pltpu.VMEM(p.shape, F32),
            pltpu.VMEM(q.shape, BF16),
            pltpu.SemaphoreType.DMA((4,)),
            pltpu.SemaphoreType.DMA((4,)),
        ],
        compiler_params=pltpu.CompilerParams(vmem_limit_bytes=20 * 2**20),
        cost_estimate=pl.CostEstimate(flops=1_000_000, bytes_accessed=5_000_000, transcendentals=0),
        name="solve_rows",
    )(pos, mine, other, *factors)


def update_kernel(pos_ref, a_hbm, p_hbm, q_hbm, gc_ref, o_hbm, a_ref, q_ref, g_ref, o_ref, load_sems, store_sems, panel_sem):
    r = pos_ref[0]
    c = pos_ref[1]
    n = 2 * NB
    order = (3, 2, 1, 0)
    part = [slice(k * NB, (k + 1) * NB) for k in range(4)]
    loads = {
        k: [
            pltpu.make_async_copy(q_hbm.at[part[k]], q_ref.at[part[k]], load_sems.at[0, k]),
            pltpu.make_async_copy(a_hbm.at[part[k]], a_ref.at[part[k]], load_sems.at[1, k]),
        ]
        for k in order
    }
    for copy in loads[3]:
        copy.start()
    panel = pltpu.make_async_copy(p_hbm, o_ref.at[:, :NB], panel_sem)

    @pl.when(c < 2)
    def _():
        panel.start()

    for k in order[1:]:
        for copy in loads[k]:
            copy.start()

    def block(k, m):
        small = dot_nt_16(q_ref[part[k], :], g_ref[part[m], :])
        small += dot_nt_16(q_ref[part[k], :2 * n], g_ref[part[m], n:])
        main = dot_nt_16(q_ref[part[k], :n], g_ref[part[m], 2 * n:])
        o_ref[part[k], part[m]] = a_ref[part[k], part[m]] - (small + main)

    def clear(k, m):
        o_ref[part[k], part[m]] = jnp.zeros((NB, NB), F32)

    def split(m):
        core = c % 2
        for h, lane in enumerate((core, 1 - core)):
            hi, mid, lo = split3(gc_ref[:, lane, m].reshape(NB, NB))
            for k, piece in enumerate((lo, mid, hi)):
                g_ref[part[m], k * n + h * NB:k * n + (h + 1) * NB] = piece.astype(BF16)

    split(1)
    for m in range(1, 4):
        for k in range(m):
            clear(k, m)

    stores = []
    for k in order:
        for copy in loads[k]:
            copy.wait()
        for m in range(1, k):
            block(k, m)
            if k == 3:
                split(m + 1)

        @pl.when(c >= 2)
        def _():
            if k == 3:
                split(0)
            if k > 0:
                block(k, 0)

        if k == 3:
            @pl.when(c < 2)
            def _():
                panel.wait()

        inside = r >= c if k > 0 else (r >= c) & (c >= 2)
        outside = r < c if k > 0 else (r < c) & (c >= 2)

        @pl.when(inside)
        def _():
            block(k, k)

        @pl.when(outside)
        def _():
            clear(k, k)

        stores.append(pltpu.make_async_copy(o_ref.at[part[k]], o_hbm.at[part[k]], store_sems.at[k]))
        stores[-1].start()
    for copy in stores:
        copy.wait()


def update(pos, a, p, q, gc):
    hbm = pl.BlockSpec(memory_space=pltpu.HBM)
    return pl.pallas_call(
        update_kernel,
        out_shape=jax.ShapeDtypeStruct(a.shape, F32),
        in_specs=[SMEM, hbm, hbm, hbm, VMEM],
        out_specs=hbm,
        scratch_shapes=[
            pltpu.VMEM(a.shape, F32),
            pltpu.VMEM(q.shape, BF16),
            pltpu.VMEM(q.shape, BF16),
            pltpu.VMEM(a.shape, F32),
            pltpu.SemaphoreType.DMA((2, 4)),
            pltpu.SemaphoreType.DMA((4,)),
            pltpu.SemaphoreType.DMA(()),
        ],
        compiler_params=pltpu.CompilerParams(vmem_limit_bytes=32 * 2**20),
        cost_estimate=pl.CostEstimate(flops=8_000_000_000, bytes_accessed=13_000_000, transcendentals=0),
        name="update",
    )(pos, a, p, q, gc)


TREE = (
    tuple(((0, d or 4),) for d in range(8)),
    (
        ((0, 6), (4, 2)), ((0, 6), (1, 3)), ((0, 6), (2, 4)), ((0, 6), (3, 5)),
        ((0, 2), (4, 6)), ((0, 2), (5, 3)), ((0, 2), (6, 4)), ((0, 2), (7, 5)),
    ),
    (
        ((0, 7), (6, 5), (4, 3), (2, 1)), ((0, 7), (1, 2), (3, 4), (6, 5)),
        ((0, 1), (2, 3), (4, 5), (6, 7)), ((0, 1), (3, 2), (5, 4), (6, 7)),
        ((0, 1), (2, 3), (4, 5), (6, 7)), ((0, 7), (2, 1), (3, 4), (5, 6)),
        ((0, 1), (2, 3), (4, 5), (6, 7)), ((0, 1), (2, 3), (5, 4), (7, 6)),
    ),
)


LEAD = (((0, 5),), ((0, 7), (5, 3)), ((0, 1), (7, 6), (5, 4), (3, 2)))


def along_z(x, moves):
    pairs = [(16 * r + 2 * a + h, 16 * r + 2 * b + h) for r in range(16) for a, b in moves(r // 2) for h in range(2)]
    return lax.ppermute(x, ("row", "col"), pairs)


def per_device(a):
    r = lax.axis_index("row").astype(jnp.int32)
    c = lax.axis_index("col").astype(jnp.int32)
    pos = jnp.stack([r, c])
    swap = [(i, i ^ 1) for i in range(16)]
    x = a[:, :NB]
    here = c < 2

    lead = lax.all_to_all(x[:NB].reshape(16, 16, NB), "row", 0, 0, tiled=True)[0:2].reshape(32, NB)
    lead = jnp.where(here, lead, 0.0)
    for moves in LEAD:
        lead += along_z(lead, lambda d: moves if d < 5 else [((8 - s) % 8, (8 - t) % 8) for s, t in moves])
    panel = jnp.where(here, x, 0.0)
    panel += along_z(panel, lambda d: TREE[0][d])
    lead, panel, pos = lax.optimization_barrier((lead, panel, pos))

    pieces = panel.reshape(4, 16, 16, NB).transpose(1, 0, 2, 3).reshape(16, 64, NB)
    pieces = jnp.concatenate([pieces, jnp.broadcast_to(lead[None], (16, 32, NB))], axis=1)
    held = lax.all_to_all(pieces, "row", 0, 0, tiled=True)
    arrived, pos = lax.optimization_barrier((along_z(panel, lambda d: TREE[1][d]), meanwhile(pos)))
    panel += arrived
    arrived = along_z(panel, lambda d: TREE[2][d])
    held, panel, pos = lax.optimization_barrier((held, panel, pos))

    lead = held[:, 64:].reshape(16, 2, 16, NB)
    theirs = lax.ppermute(lead, "col", swap)
    mine = lax.dynamic_index_in_dim(held, c, 0, keepdims=False)[:64]
    other = lax.ppermute(lax.dynamic_index_in_dim(held, c ^ 1, 0, keepdims=False)[:64], "col", swap)
    mine, other, lead, theirs, panel = lax.optimization_barrier((mine, other, lead, theirs, panel))
    gc = jnp.stack([mine, other]).reshape(2, 4, 16, NB)
    gc = lax.all_to_all(jnp.broadcast_to(gc[None], (16, 2, 4, 16, NB)), "row", 0, 0, tiled=True)
    *factors, arrived = lax.optimization_barrier((*factor(pos, lead, theirs), arrived))
    panel += arrived
    p, q = solve_rows(pos, panel, lax.ppermute(panel, "col", swap), factors)
    a, p, q = (pltpu.with_memory_space_constraint(v, pltpu.HBM) for v in (a, p, q))
    return update(pos, a, p, q, gc)


def solution(mesh):
    return jax.shard_map(
        per_device,
        mesh=mesh,
        in_specs=(P("row", "col"),),
        out_specs=P("row", "col"),
        check_vma=False,
    )
```
